512 devices in a mesh: region: 4 (over x), tile: 16 (over z), link: 8 (over y, core).
Axes of the slice: x: 4, y: 4, z: 16, core: 2. Of those that a mesh axis runs over, the one named last changes fastest.
Arguments:
- tiles: bfloat16 [4, 16, 64, 256, 256], P('region', 'tile', 'link'), may hold values from -0.1875 to 0.1875
- tile_row: int32 [4, 16, 64], P('region', 'tile', 'link'), may hold values from 0 to 15
- tile_col: int32 [4, 16, 64], P('region', 'tile', 'link'), may hold values from 0 to 7
- tile_count: int32 [4, 16, 8], P('region', 'tile', 'link'), may hold values from 1 to 8, 33 in all within a row
- linkage_tiles: bfloat16 [4, 16, 8, 256, 256], P('region', 'tile', 'link'), may hold values from -0.046875 to 0.046875
- linkage_block: int32 [4, 16, 8], P('region', 'tile', 'link'), may hold values from 0 to 7
- column_cost: float32 [131072], P(('region', 'tile', 'link')), may hold values from -6 to 6
- capacity_cost: float32 [2048], P('link'), may hold values from -6 to 6
- demand: float32 [32, 131072], P(None, ('region', 'tile', 'link')), may hold values from -6 to 6
- linkage_bound: float32 [2048], P('link'), may hold values from -6 to 6
- primal_now: float32 [32, 131072], P(None, ('region', 'tile', 'link')), may hold values from 0 to 2
- capacity_now: float32 [32, 2048], P(None, 'link'), may hold values from 0 to 2
- duals_now: float32 [32, 131072], P(None, ('region', 'tile', 'link')), may hold values from 0 to 2
- linkage_now: float32 [32, 2048], P(None, 'link'), may hold values from 0 to 2
- primal_mean: float32 [32, 131072], P(None, ('region', 'tile', 'link')), may hold values from 0 to 2
- capacity_mean: float32 [32, 2048], P(None, 'link'), may hold values from 0 to 2
- duals_mean: float32 [32, 131072], P(None, ('region', 'tile', 'link')), may hold values from 0 to 2
- linkage_mean: float32 [32, 2048], P(None, 'link'), may hold values from 0 to 2
- restart: int32 [32], replicated, may hold values from 0 to 1
- mean_count: int32 [32], replicated, may hold values from 1 to 8
- primal_step: float32 [32], replicated, may hold values from 0.1 to 0.4
- dual_step: float32 [32], replicated, may hold values from 0.1 to 0.4
Outputs:
- primal_next: float32 [32, 131072], P(None, ('region', 'tile', 'link'))
- capacity_next: float32 [32, 2048], P(None, 'link')
- duals_next: float32 [32, 131072], P(None, ('region', 'tile', 'link'))
- linkage_next: float32 [32, 2048], P(None, 'link')
- primal_average: float32 [32, 131072], P(None, ('region', 'tile', 'link'))
- capacity_average: float32 [32, 2048], P(None, 'link')
- duals_average: float32 [32, 131072], P(None, ('region', 'tile', 'link'))
- linkage_average: float32 [32, 2048], P(None, 'link')
- movement: float32 [32], replicated
The draws below stay inside these ranges and needn't reach their ends.
Inputs may be any that keep to these rules, and one draw needn't show every extreme that they name: `tile_count`: each region and tile index has one device holding exactly 8 live slots; slots at or past a device's count are ignored. `restart`: 1 restarts a scenario from its averages.
All inputs are finite; a program needn't handle non-finite values.
Results may differ from the reference program's by a relative error of at most 0.0013.
Values may be sent and summed in bfloat16 or wider, within the bound.
A program may use at most 64 MiB of HBM per device.

```python
import math
import jax
import jax.numpy as jnp
import numpy as np
from jax import lax

BLOCK = 256
SCEN = 32
TILES_DEV = 8
REGIONS = 4
NCOLS = 131072
NROWS = 131072
LROWS = 2048
N_TILE = 16
N_LINK = 8


def place_ends(drawn, own_key, smallest, largest):
    dims = drawn.shape
    index_at = [jax.random.randint(jax.random.fold_in(own_key, axis), (), 0, dims[axis]) for axis in range(len(dims))]
    drawn = drawn.at[tuple(index_at)].set(smallest)
    longest = dims.index(max(dims))
    index_at[longest] = (index_at[longest] + 1) % dims[longest]
    return drawn.at[tuple(index_at)].set(largest)


def steps_of(rng, dims, cuts, least, top_value):
    def one(axis_at, blocks):
        heights = jax.random.uniform(jax.random.fold_in(jax.random.fold_in(rng, 6), axis_at), (blocks,), jnp.float32, least / len(cuts), top_value / len(cuts))
        return jnp.repeat(jnp.exp(heights), dims[axis_at] // blocks).reshape((-1,) + (1,) * (len(dims) - axis_at - 1))

    gain = one(*cuts[0])
    for cut in cuts[1:]:
        gain = gain * one(*cut)
    return gain


def length_profile(number_of, total, reach, skew):
    weights = [(1 << 20) // math.isqrt(standing ** skew) + 1 for standing in range(2, number_of + 1)]
    surplus, given = total - reach - (number_of - 1), [1] * (number_of - 1)
    while surplus > 0:
        movable = [i for i in range(number_of - 1) if given[i] < reach]
        whole, left = sum([weights[i] for i in movable]), surplus
        for i in movable:
            extra = min(reach - given[i], max(1, left * weights[i] // whole), surplus)
            given[i] = given[i] + extra
            surplus = surplus - extra
    return np.array([reach] + given)


def ragged(key, amount, total, bound, skew):
    if amount == 2:
        one = jax.random.randint(key, (), max(1, total - bound), min(bound, total - 1) + 1)
        return jnp.stack([one, total - one])
    sizes = jnp.asarray(length_profile(amount, total, bound, skew), jnp.int32)
    couples = (amount - 1) // 2
    source_of, taker = sizes[1:1 + 2 * couples:2], sizes[2:2 + 2 * couples:2]
    slack = jnp.minimum(source_of - 1, bound - taker)
    passed = jax.random.randint(jax.random.fold_in(key, 1), (couples,), 0, 1 << 20) % (slack + 1)
    sizes = sizes.at[1:1 + 2 * couples:2].set(source_of - passed).at[2:2 + 2 * couples:2].set(taker + passed)
    return sizes[jax.random.permutation(jax.random.fold_in(key, 2), amount)]


def normal_values(rng, extent, spread, reach, pieces=(), kind=jnp.bfloat16):
    factor_of = steps_of(rng, extent, pieces, -0.22, 0.18) if pieces else 1.0
    array = jax.random.normal(rng, extent, jnp.float32) * spread * factor_of
    return jnp.minimum(jnp.maximum(array, -reach), reach).astype(kind)


def setup_inputs(seed: int = 0) -> dict:
    key_list = jax.random.split(jax.random.key(seed), 23)
    tiles = normal_values(key_list[0], (REGIONS, N_TILE, N_LINK * TILES_DEV, BLOCK, BLOCK), (BLOCK * TILES_DEV // 2) ** -0.5, 0.1875, ((0, 4), (1, 16), (2, 8)))
    tile_row = place_ends(jax.random.randint(key_list[1], (REGIONS, N_TILE, N_LINK * TILES_DEV), 0, N_TILE), jax.random.fold_in(key_list[1], 1), 0, N_TILE - 1).astype(jnp.int32)
    tile_col = place_ends(jax.random.randint(key_list[2], (REGIONS, N_TILE, N_LINK * TILES_DEV), 0, N_LINK), jax.random.fold_in(key_list[2], 1), 0, N_LINK - 1).astype(jnp.int32)
    tile_count = jax.vmap(lambda own: ragged(own, N_LINK, N_LINK * TILES_DEV // 2 + 1, TILES_DEV, 2))(jax.random.split(key_list[3], REGIONS * N_TILE)).reshape((REGIONS, N_TILE, N_LINK)).astype(jnp.int32)
    linkage_tiles = normal_values(key_list[4], (REGIONS, N_TILE, N_LINK, BLOCK, BLOCK), (BLOCK * REGIONS * N_TILE) ** -0.5, 0.046875, ((0, 4), (1, 16), (2, 8)))
    linkage_block = place_ends(jax.random.randint(key_list[5], (REGIONS, N_TILE, N_LINK), 0, N_LINK), jax.random.fold_in(key_list[5], 1), 0, N_LINK - 1).astype(jnp.int32)
    column_cost = normal_values(key_list[6], (NCOLS,), 1.0, 6.0, ((0, 512),), jnp.float32)
    capacity_cost = normal_values(key_list[7], (LROWS,), 1.0, 6.0, ((0, 8),), jnp.float32)
    demand = normal_values(key_list[8], (SCEN, NROWS), 1.0, 6.0, ((1, 512),), jnp.float32)
    linkage_bound = normal_values(key_list[9], (LROWS,), 1.0, 6.0, ((0, 8),), jnp.float32)
    primal_now = jnp.clip(2.0 * jax.random.uniform(key_list[10], (SCEN, NCOLS), jnp.float32) ** steps_of(key_list[10], (SCEN, NCOLS), ((1, 512),), -0.2, 0.2), 0.0, 2.0)
    capacity_now = jnp.clip(2.0 * jax.random.uniform(key_list[11], (SCEN, LROWS), jnp.float32) ** steps_of(key_list[11], (SCEN, LROWS), ((1, 8),), -0.2, 0.2), 0.0, 2.0)
    duals_now = jnp.clip(2.0 * jax.random.uniform(key_list[12], (SCEN, NROWS), jnp.float32) ** steps_of(key_list[12], (SCEN, NROWS), ((1, 512),), -0.2, 0.2), 0.0, 2.0)
    linkage_now = jnp.clip(2.0 * jax.random.uniform(key_list[13], (SCEN, LROWS), jnp.float32) ** steps_of(key_list[13], (SCEN, LROWS), ((1, 8),), -0.2, 0.2), 0.0, 2.0)
    primal_mean = jnp.clip(2.0 * jax.random.uniform(key_list[14], (SCEN, NCOLS), jnp.float32) ** steps_of(key_list[14], (SCEN, NCOLS), ((1, 512),), -0.2, 0.2), 0.0, 2.0)
    capacity_mean = jnp.clip(2.0 * jax.random.uniform(key_list[15], (SCEN, LROWS), jnp.float32) ** steps_of(key_list[15], (SCEN, LROWS), ((1, 8),), -0.2, 0.2), 0.0, 2.0)
    duals_mean = jnp.clip(2.0 * jax.random.uniform(key_list[16], (SCEN, NROWS), jnp.float32) ** steps_of(key_list[16], (SCEN, NROWS), ((1, 512),), -0.2, 0.2), 0.0, 2.0)
    linkage_mean = jnp.clip(2.0 * jax.random.uniform(key_list[17], (SCEN, LROWS), jnp.float32) ** steps_of(key_list[17], (SCEN, LROWS), ((1, 8),), -0.2, 0.2), 0.0, 2.0)
    restart = place_ends(jax.random.randint(key_list[18], (SCEN,), 0, 2), jax.random.fold_in(key_list[18], 1), 0, 1).astype(jnp.int32)
    mean_count = place_ends(jax.random.randint(key_list[19], (SCEN,), 1, 9), jax.random.fold_in(key_list[19], 1), 1, 8).astype(jnp.int32)
    primal_step = jnp.clip(jnp.exp(jax.random.uniform(key_list[20], (SCEN,), jnp.float32, math.log(0.1), math.log(0.4))), 0.1, 0.4)
    dual_step = jnp.clip(jnp.exp(jax.random.uniform(key_list[21], (SCEN,), jnp.float32, math.log(0.1), math.log(0.4))), 0.1, 0.4)
    return dict(tiles=tiles, tile_row=tile_row, tile_col=tile_col, tile_count=tile_count, linkage_tiles=linkage_tiles, linkage_block=linkage_block, column_cost=column_cost, capacity_cost=capacity_cost, demand=demand, linkage_bound=linkage_bound, primal_now=primal_now, capacity_now=capacity_now, duals_now=duals_now, linkage_now=linkage_now, primal_mean=primal_mean, capacity_mean=capacity_mean, duals_mean=duals_mean, linkage_mean=linkage_mean, restart=restart, mean_count=mean_count, primal_step=primal_step, dual_step=dual_step)


HIGH = lax.Precision.HIGHEST


def reference(tiles, tile_row, tile_col, tile_count, linkage_tiles, linkage_block, column_cost, capacity_cost, demand, linkage_bound, primal_now, capacity_now, duals_now, linkage_now, primal_mean, capacity_mean, duals_mean, linkage_mean, restart, mean_count, primal_step, dual_step):
    slabs = tiles.reshape(REGIONS, N_TILE, N_LINK, TILES_DEV, BLOCK, BLOCK)
    row_ids = tile_row.reshape(REGIONS, N_TILE, N_LINK, TILES_DEV)
    column_ids = tile_col.reshape(REGIONS, N_TILE, N_LINK, TILES_DEV)
    active = (jnp.arange(TILES_DEV, dtype=jnp.int32)[None, None, None, :] < tile_count[..., None]).astype(jnp.float32)
    row_pick = (row_ids[..., None] == jnp.arange(N_TILE, dtype=jnp.int32)).astype(jnp.float32) * active[..., None]
    column_pick = (column_ids[..., None] == jnp.arange(N_LINK, dtype=jnp.int32)).astype(jnp.float32) * active[..., None]
    lanes = jnp.broadcast_to(jnp.arange(N_LINK, dtype=jnp.int32)[:, None], (N_LINK, TILES_DEV))
    link_slabs = linkage_tiles.astype(jnp.float32)
    link_pick = (linkage_block[..., None] == jnp.arange(N_LINK, dtype=jnp.int32)).astype(jnp.float32)

    def forward_regional(extrap):
        values = extrap.astype(jnp.float32).reshape(SCEN, REGIONS, N_TILE, N_LINK, BLOCK).transpose(1, 2, 0, 3, 4)

        def region_rows(items):
            def tile_step(total, inner):
                slab_t, ids_t, pick_t, values_t = inner
                picked = jnp.take(values_t, ids_t, axis=1)
                terms = jnp.einsum('slkj,lkij->slki', picked, slab_t.astype(jnp.float32), precision=HIGH)
                return total + jnp.einsum('slki,lkp->spli', terms, pick_t, precision=HIGH), None
            total, _ = lax.scan(tile_step, jnp.zeros((SCEN, N_TILE, N_LINK, BLOCK), jnp.float32), items)
            return total

        sums = lax.map(region_rows, (slabs, column_ids, row_pick, values))
        return sums.transpose(1, 0, 2, 3, 4).reshape(SCEN, NROWS)

    def transpose_regional(duals_low):
        values = duals_low.astype(jnp.float32).reshape(SCEN, REGIONS, N_TILE, N_LINK, BLOCK).transpose(1, 0, 2, 3, 4)

        def region_columns(items):
            slabs_r, ids_r, pick_r, values_r = items

            def tile_columns(inner):
                slab_t, ids_t, pick_t = inner
                picked = values_r[:, ids_t, lanes]
                terms = jnp.einsum('slki,lkij->slkj', picked, slab_t.astype(jnp.float32), precision=HIGH)
                return jnp.einsum('slkj,lkc->scj', terms, pick_t, precision=HIGH)
            return lax.map(tile_columns, (slabs_r, ids_r, pick_r))

        sums = lax.map(region_columns, (slabs, row_ids, column_pick, values))
        return sums.transpose(2, 0, 1, 3, 4).reshape(SCEN, NCOLS)

    def forward_linkage(extrap):
        values = extrap.astype(jnp.float32).reshape(SCEN, REGIONS, N_TILE, N_LINK, BLOCK)
        terms = jnp.einsum('srtlj,rtlij->srtli', values, link_slabs, precision=HIGH)
        return jnp.einsum('srtli,rtlm->smi', terms, link_pick, precision=HIGH).reshape(SCEN, LROWS)

    def transpose_linkage(linkage_low):
        values = linkage_low.astype(jnp.float32).reshape(SCEN, N_LINK, BLOCK)
        picked = values[:, linkage_block]
        return jnp.einsum('srtli,rtlij->srtlj', picked, link_slabs, precision=HIGH).reshape(SCEN, NCOLS)

    restarted = (restart == 1)[:, None]
    primal = jnp.where(restarted, primal_mean, primal_now)
    capacity = jnp.where(restarted, capacity_mean, capacity_now)
    duals = jnp.where(restarted, duals_mean, duals_now)
    linkage = jnp.where(restarted, linkage_mean, linkage_now)
    starts = (primal, capacity, duals, linkage)
    step_p = primal_step[:, None]
    step_d = dual_step[:, None]
    history = []
    for sweep in range(2):
        gradient = transpose_regional(duals.astype(jnp.bfloat16)) - transpose_linkage(linkage.astype(jnp.bfloat16))
        primal_new = jnp.maximum(primal - step_p * (column_cost[None, :] - gradient), 0.0)
        capacity_new = jnp.maximum(capacity - step_p * (capacity_cost[None, :] - linkage), 0.0)
        extrap = (2.0 * primal_new - primal).astype(jnp.bfloat16)
        capacity_bar = 2.0 * capacity_new - capacity
        duals_new = jnp.maximum(duals + step_d * (demand - forward_regional(extrap)), 0.0)
        linkage_new = jnp.maximum(linkage + step_d * (linkage_bound[None, :] - (capacity_bar - forward_linkage(extrap))), 0.0)
        primal, capacity, duals, linkage = primal_new, capacity_new, duals_new, linkage_new
        history.append((primal, capacity, duals, linkage))
    weight = (mean_count * (1 - restart)).astype(jnp.float32)[:, None]
    means = (primal_mean, capacity_mean, duals_mean, linkage_mean)
    averages = [(weight * means[i] + history[0][i] + history[1][i]) / (weight + 2.0) for i in range(4)]
    movement = jnp.zeros((SCEN,), jnp.float32)
    for i in range(4):
        movement = movement + jnp.sum((history[1][i] - starts[i]) ** 2, axis=1)
    return (history[1][0], history[1][1], history[1][2], history[1][3], averages[0], averages[1], averages[2], averages[3], movement)
```

```python
import types

import jax
import jax.numpy as jnp
from jax import lax
from jax.experimental import pallas as pl
from jax.experimental.pallas import tpu as pltpu
from jax.sharding import PartitionSpec as P

REGION, TILE, LINK = SPLIT = ("region", "tile", "link")
MESH = pl.DeviceIdType.MESH
F32 = jnp.float32
BF16 = jnp.bfloat16
HALVES = 2
SWEEPS = 2
NEAR = (1, -1, 2, -2)
FAR = 5
N_SEMS = 280
VMEM_LIMIT = 62 * 1024 * 1024
Z_PARTNERS = (FAR, -FAR, 3, -3, 2, -2, 1, -1)


def dot_nn(a, b):
    return lax.dot_general(a, b, (((1,), (0,)), ((), ())), preferred_element_type=F32)


def dot_nt(a, b):
    return lax.dot_general(a, b, (((1,), (1,)), ((), ())), preferred_element_type=F32)


def kernel(n_region, n_tile, n_link, out, moved_out, refs):
    r, t, l = lax.axis_index(REGION), lax.axis_index(TILE), lax.axis_index(LINK)
    tile_row, tile_col, tile_count, linkage_block = refs.rows, refs.cols, refs.count, refs.target
    scen, width = refs.y.shape[1:]
    slots = refs.tiles_v.shape[0]
    half = scen // HALVES
    piece = scen // n_region
    ssem, rsem = refs.ssem, refs.rsem
    used = [0]
    sent = []

    def z_dev(offset):
        return (r, lax.rem(t + (offset + n_tile), n_tile), l)

    def link_dev(offset):
        return (r, t, lax.rem(l + offset, n_link))

    def region_dev(offset):
        return (lax.rem(r + offset, n_region), t, l)

    def send(src, dst, dev):
        i = used[0]
        used[0] = i + 1
        assert i < N_SEMS
        c = pltpu.make_async_remote_copy(
            src_ref=src, dst_ref=dst, send_sem=ssem.at[i], recv_sem=rsem.at[i], device_id=dev, device_id_type=MESH
        )
        c.start()
        sent.append(c)
        return c

    barrier = pltpu.get_barrier_semaphore()
    for o in Z_PARTNERS:
        pl.semaphore_signal(barrier, inc=1, device_id=z_dev(o), device_id_type=MESH)
    for o in range(1, n_link):
        pl.semaphore_signal(barrier, inc=1, device_id=link_dev(o), device_id_type=MESH)
    for o in range(1, n_region):
        pl.semaphore_signal(barrier, inc=1, device_id=region_dev(o), device_id_type=MESH)

    def load(i, src, dst):
        c = pltpu.make_async_copy(src, dst, refs.lsem.at[i])
        c.start()
        return c

    duals_loads = [load(0, refs.duals_now, refs.duals_now_v), load(1, refs.duals_mean, refs.duals_mean_v)]
    linkage_loads = [load(2, refs.linkage_now, refs.linkage_now_v), load(3, refs.linkage_mean, refs.linkage_mean_v)]
    other_loads = [
        load(4, refs.tiles, refs.tiles_v),
        load(5, refs.ltile, refs.ltile_v),
        load(6, refs.demand, refs.demand_v),
        load(7, refs.primal_now, refs.primal_now_v),
        load(8, refs.primal_mean, refs.primal_mean_v),
        load(9, refs.capacity_now, refs.capacity_now_v),
        load(10, refs.capacity_mean, refs.capacity_mean_v),
    ]

    eye = lax.broadcasted_iota(jnp.int32, (scen, scen), 0) == lax.broadcasted_iota(jnp.int32, (scen, scen), 1)

    def column(row):
        return jnp.sum(jnp.where(eye, jnp.broadcast_to(row, (scen, scen)), 0.0), axis=1, keepdims=True)

    restart_row = refs.restart[...].astype(F32)
    restarted = jnp.broadcast_to(column(restart_row), (scen, width)) == 1.0
    weight = jnp.broadcast_to(column(refs.mean_count[...].astype(F32) * (1.0 - restart_row)), (scen, width))
    step_p = jnp.broadcast_to(column(refs.primal_step[...]), (scen, width))
    step_d = jnp.broadcast_to(column(refs.dual_step[...]), (scen, width))

    def part(value, h):
        return value[h * half : (h + 1) * half]

    def rows_of(h):
        return pl.ds(h * half, half)

    live = tile_count[0, 0, 0]
    row_at, col_at = [], []
    for k in range(slots):
        dead = jnp.where(k < live, 0, -64)
        row_at.append(lax.rem(tile_row[0, 0, k] - t + n_tile, n_tile) + dead)
        col_at.append(lax.rem(tile_col[0, 0, k] - l + n_link, n_link) + dead)
    row_slot = [lax.rem(tile_row[0, 0, k] - t + n_tile, n_tile) for k in range(slots)]
    col_slot = [lax.rem(tile_col[0, 0, k] - l + n_link, n_link) for k in range(slots)]
    target_at = lax.rem(linkage_block[0, 0, 0] - l + n_link, n_link)

    x, y, z, w = refs.x, refs.y, refs.z, refs.w
    for c in duals_loads:
        c.wait()
    y[0] = jnp.where(restarted, refs.duals_mean_v[...], refs.duals_now_v[...])
    for h in range(HALVES):
        refs.yg[0][h][0] = y[0, rows_of(h), :].astype(BF16)
    for c in linkage_loads:
        c.wait()
    w[0] = jnp.where(restarted, refs.linkage_mean_v[...], refs.linkage_now_v[...])
    refs.wg[0][0] = w[0].astype(BF16)

    pl.semaphore_wait(barrier, len(Z_PARTNERS) + n_link - 1 + n_region - 1)

    def duals_send(s, h):
        g = refs.yg[s][h]
        out = {}
        for d in (FAR, -FAR) + NEAR:
            slot = -d % n_tile
            out[slot] = send(g.at[0], g.at[slot], z_dev(d))
        return out

    def duals_forward(s, h, out):
        g = refs.yg[s][h]
        order = (-3, -2, -1, 1, 2) if h == 0 else (-2, -1, 1, 2)
        back = (3, 2, 1, -1, -2) if h == 1 else (2, 1, -1, -2)
        for slot, moves in ((FAR, order), (n_tile - FAR, back)):
            out.pop(slot).wait_recv()
            for d in moves:
                to = (slot - d) % n_tile
                out[to] = send(g.at[slot], g.at[to], z_dev(d))

    def link_gather(buf):
        out = []
        for d in range(1, n_link):
            out.append(send(buf.at[0], buf.at[-d % n_link], link_dev(d)))
        return out

    def finish(copies):
        for c in copies:
            c.wait_recv()

    def picked(at, terms, offset):
        total = None
        for k in range(slots):
            one = jnp.where(at[k] == offset, 1.0, 0.0) * terms[k]
            total = one if total is None else total + one
        return total

    def columns_send(s, h):
        g = refs.yg[s][h]
        terms = [dot_nn(g[row_slot[k]], refs.tiles_v[k]) for k in range(slots)]
        out = refs.cout[s][h]
        copies = []
        for o in list(range(1, n_link)) + [0]:
            out[o] = picked(col_at, terms, o)
            if o:
                copies.append(send(out.at[o], refs.cin[s][h].at[o], link_dev(o)))
        return copies

    def primal_update(s, h):
        total = refs.cout[s][h][0]
        for o in range(1, n_link):
            total = total + refs.cin[s][h][o]
        linked = refs.wg[s][target_at]
        gradient = total - dot_nn(part(linked, h), refs.ltile_v[...])
        old = x[s, rows_of(h), :]
        new = jnp.maximum(old - part(step_p, h) * (refs.column_cost[...] - gradient), 0.0)
        x[s + 1, rows_of(h), :] = new
        extrap = (2.0 * new - old).astype(BF16)
        refs.eg[s][h][0] = extrap

    def rows_send(s, h):
        g = refs.eg[s][h]
        terms = [dot_nt(g[col_slot[k]], refs.tiles_v[k]) for k in range(slots)]
        out, near = refs.rout[s][h], refs.rnear[s][h]
        third = 3 if h == 0 else -3
        relay, direct = [], []
        for i, e in enumerate(NEAR):
            out[i, 0] = picked(row_at, terms, (-e - FAR) % n_tile)
            out[i, 1] = picked(row_at, terms, (-e + FAR) % n_tile)
            relay.append(send(out.at[i], refs.rin[s][h].at[i], z_dev(-e)))
            if i == 0:
                out[4, 0] = picked(row_at, terms, n_tile // 2)
                relay.append(send(out.at[4, 0], refs.rin[s][h].at[4, 0], z_dev(-third)))
        for i, e in enumerate(NEAR):
            near[i] = picked(row_at, terms, -e % n_tile)
        near[4] = picked(row_at, terms, n_tile - FAR)
        near[5] = picked(row_at, terms, FAR)
        near[6] = picked(row_at, terms, 0)
        return relay, direct

    def rows_direct(s, h, direct):
        for i, e in enumerate(NEAR):
            direct.append(send(refs.rnear[s][h].at[i], refs.rdir[s][h].at[i], z_dev(-e)))

    def rows_relay(s, h, relay, direct):
        finish(relay)
        got, near = refs.rin[s][h], refs.rnear[s][h]
        for j in range(2):
            total = near[4 + j]
            for i in range(4):
                total = total + got[i, j]
            if j == h:
                total = total + got[4, 0]
            near[4 + j] = total
            direct.append(send(near.at[4 + j], refs.rdir[s][h].at[4 + j], z_dev(FAR if j else -FAR)))

    def duals_update(s, h, direct):
        finish(direct)
        total = refs.rnear[s][h][6]
        for i in range(6):
            total = total + refs.rdir[s][h][i]
        rows = rows_of(h)
        new = jnp.maximum(y[s, rows, :] + part(step_d, h) * (refs.demand_v[rows, :] - total), 0.0)
        y[s + 1, rows, :] = new
        if s + 1 < SWEEPS:
            refs.yg[s + 1][h][0] = new.astype(BF16)

    def linking_start(s):
        out = refs.lout[s]
        e = jnp.concatenate([refs.eg[s][h][0] for h in range(HALVES)], axis=0)
        term = dot_nt(e, refs.ltile_v[...])
        copies = []
        for o in list(range(1, n_link)) + [0]:
            out[o] = jnp.where(target_at == o, 1.0, 0.0) * term
            if o:
                copies.append(send(out.at[o], refs.lin[s].at[o], link_dev(o)))
        return copies

    def linking_region(s, copies):
        finish(copies)
        total = refs.lout[s][0]
        for o in range(1, n_link):
            total = total + refs.lin[s][o]
        own = refs.lsum[s]
        own[...] = total
        got = refs.lreg[s]
        result = []
        for o in range(1, n_region):
            to = lax.rem(r + o, n_region)
            rows = pl.ds(pl.multiple_of(to * piece, piece), piece)
            result.append(send(own.at[rows, :], got.at[r], region_dev(o)))
        got[r] = own[pl.ds(pl.multiple_of(r * piece, piece), piece), :]
        return result

    def summed(ref, n):
        total = ref[0]
        for i in range(1, n):
            total = total + ref[i]
        return total

    def spread(buf, at, value, devs):
        buf[at] = value
        return [send(buf.at[at], buf.at[at], d) for d in devs]

    region_devs = [region_dev(o) for o in range(1, n_region)]
    link_devs = [link_dev(o) for o in range(1, n_link)]

    def z_spread(buf, value):
        buf[t] = value
        return {d: send(buf.at[t], buf.at[t], z_dev(-d)) for d in (FAR, -FAR) + NEAR}

    def z_relay(buf, out):
        for d, moves in ((FAR, (-3, -2, -1, 1, 2)), (-FAR, (2, 1, -1, -2))):
            out.pop(d).wait_recv()
            at = lax.rem(t + (d + n_tile), n_tile)
            for m in moves:
                out[d, m] = send(buf.at[at], buf.at[at], z_dev(m))

    def linking_z(s, copies):
        finish(copies)
        return z_spread(refs.lz[s], summed(refs.lreg[s], n_region))

    def linking_back(s, copies):
        finish(copies.values())
        return spread(refs.lback[s], r, summed(refs.lz[s], n_tile), region_devs)

    def capacity_update(s):
        z[s + 1] = jnp.maximum(z[s] - step_p * (refs.capacity_cost[...] - w[s]), 0.0)

    def linking_update(s, copies):
        finish(copies)
        back = refs.lback[s]
        total = jnp.concatenate([back[i] for i in range(n_region)], axis=0)
        bar = 2.0 * z[s + 1] - z[s]
        w[s + 1] = jnp.maximum(w[s] + step_d * (refs.linkage_bound[...] - (bar - total)), 0.0)

    def average(mean, state, i):
        out[i] = (weight * mean + state[1] + state[2]) / (weight + 2.0)

    ready = [duals_send(0, h) for h in range(HALVES)]
    w_copies = link_gather(refs.wg[0])
    for c in other_loads:
        c.wait()
    x[0] = jnp.where(restarted, refs.primal_mean_v[...], refs.primal_now_v[...])
    z[0] = jnp.where(restarted, refs.capacity_mean_v[...], refs.capacity_now_v[...])

    link_copies = None
    for s in range(SWEEPS):
        last = s + 1 == SWEEPS
        for h in range(HALVES):
            duals_forward(s, h, ready[h])
        if s:
            link_copies = linking_back(s - 1, link_copies)
        columns = []
        for h in range(HALVES):
            finish(ready[h].values())
            columns.append(columns_send(s, h))
        if s:
            linking_update(s - 1, link_copies)
            refs.wg[s][0] = w[s].astype(BF16)
            w_copies = link_gather(refs.wg[s])
        capacity_update(s)
        finish(w_copies)
        gathers = []
        for h in range(HALVES):
            finish(columns[h])
            primal_update(s, h)
            gathers.append(link_gather(refs.eg[s][h]))
        link_copies = linking_start(s)
        relays = []
        for h in range(HALVES):
            finish(gathers[h])
            relays.append(rows_send(s, h))
        for h in range(HALVES):
            rows_direct(s, h, relays[h][1])
        link_copies = linking_region(s, link_copies)
        for h in range(HALVES):
            rows_relay(s, h, *relays[h])
        link_copies = linking_z(s, link_copies)
        if last:
            out[0] = x[2]
            out[1] = z[2]
            average(refs.primal_mean_v[...], x, 4)
            average(refs.capacity_mean_v[...], z, 5)
        for h in range(HALVES):
            duals_update(s, h, relays[h][1])
            if not last:
                ready[h] = duals_send(s + 1, h)
        z_relay(refs.lz[s], link_copies)

    def squares(state):
        return jnp.sum((state[2] - state[0]) ** 2, axis=1, keepdims=True)

    def as_row(col):
        lanes = refs.mz.shape[-1]
        on = lax.broadcasted_iota(jnp.int32, (scen, lanes), 0) == lax.broadcasted_iota(jnp.int32, (scen, lanes), 1)
        return jnp.sum(jnp.where(on, jnp.broadcast_to(col, (scen, lanes)), 0.0), axis=0, keepdims=True)

    copies = z_spread(refs.mz, as_row(squares(x) + squares(y)))
    out[2] = y[2]
    average(refs.duals_mean_v[...], y, 6)
    z_relay(refs.mz, copies)
    link_copies = linking_back(SWEEPS - 1, link_copies)
    finish(copies.values())
    copies = spread(refs.mreg, r, summed(refs.mz, n_tile), region_devs)
    linking_update(SWEEPS - 1, link_copies)
    moved = as_row(squares(z) + squares(w))
    out[3] = w[2]
    average(refs.linkage_mean_v[...], w, 7)
    finish(copies)
    copies = spread(refs.mlink, l, summed(refs.mreg, n_region) + moved, link_devs)
    finish(copies)
    moved_out[...] = summed(refs.mlink, n_link)
    for c in sent:
        c.wait_send()


def on_device(
    tiles, tile_row, tile_col, tile_count, linkage_tiles, linkage_block, column_cost, capacity_cost, demand,
    linkage_bound, primal_now, capacity_now, duals_now, linkage_now, primal_mean, capacity_mean, duals_mean,
    linkage_mean, restart, mean_count, primal_step, dual_step,
):
    n_region, n_tile, n_link = (lax.axis_size(a) for a in SPLIT)
    scen, width = primal_now.shape
    slots = tile_row.shape[2]
    half = scen // HALVES
    piece = scen // n_region
    smem = pl.BlockSpec(memory_space=pltpu.SMEM)
    vmem = pl.BlockSpec(memory_space=pltpu.VMEM)
    hbm = pl.BlockSpec(memory_space=pltpu.HBM)
    anywhere = pl.BlockSpec(memory_space=pl.ANY)
    inputs = dict(
        rows=(tile_row, smem),
        cols=(tile_col, smem),
        count=(tile_count, smem),
        target=(linkage_block, smem),
        restart=(restart.reshape(1, scen), vmem),
        mean_count=(mean_count.reshape(1, scen), vmem),
        primal_step=(primal_step.reshape(1, scen), vmem),
        dual_step=(dual_step.reshape(1, scen), vmem),
        column_cost=(column_cost.reshape(1, width), vmem),
        capacity_cost=(capacity_cost.reshape(1, width), vmem),
        linkage_bound=(linkage_bound.reshape(1, width), vmem),
        tiles=(tiles.reshape(slots, width, width), hbm),
        ltile=(linkage_tiles.reshape(width, width), hbm),
        demand=(demand, hbm),
        primal_now=(primal_now, hbm),
        capacity_now=(capacity_now, hbm),
        duals_now=(duals_now, hbm),
        linkage_now=(linkage_now, hbm),
        primal_mean=(primal_mean, hbm),
        capacity_mean=(capacity_mean, hbm),
        duals_mean=(duals_mean, hbm),
        linkage_mean=(linkage_mean, hbm),
    )
    results = jax.ShapeDtypeStruct((8, scen, width), F32)
    moved = jax.ShapeDtypeStruct((1, 128), F32)
    block = pltpu.VMEM((scen, width), F32)

    def per_sweep(shape, dtype):
        return [pltpu.VMEM(shape, dtype)] * SWEEPS

    def per_half(shape, dtype):
        return [[pltpu.VMEM(shape, dtype)] * HALVES] * SWEEPS

    scratch = dict(
        ssem=pltpu.SemaphoreType.DMA((N_SEMS,)),
        rsem=pltpu.SemaphoreType.DMA((N_SEMS,)),
        lsem=pltpu.SemaphoreType.DMA((11,)),
        tiles_v=pltpu.VMEM((slots, width, width), BF16),
        ltile_v=pltpu.VMEM((width, width), BF16),
        mz=pltpu.VMEM((n_tile, 1, 128), F32),
        mreg=pltpu.VMEM((n_region, 1, 128), F32),
        mlink=pltpu.VMEM((n_link, 1, 128), F32),
        duals_now_v=block,
        duals_mean_v=block,
        linkage_now_v=block,
        linkage_mean_v=block,
        primal_now_v=block,
        primal_mean_v=block,
        capacity_now_v=block,
        capacity_mean_v=block,
        demand_v=block,
        x=pltpu.VMEM((SWEEPS + 1, scen, width), F32),
        y=pltpu.VMEM((SWEEPS + 1, scen, width), F32),
        z=pltpu.VMEM((SWEEPS + 1, scen, width), F32),
        w=pltpu.VMEM((SWEEPS + 1, scen, width), F32),
        wg=per_sweep((n_link, scen, width), BF16),
        lout=per_sweep((n_link, scen, width), F32),
        lin=per_sweep((n_link, scen, width), F32),
        lsum=per_sweep((scen, width), F32),
        lreg=per_sweep((n_region, piece, width), F32),
        lz=per_sweep((n_tile, piece, width), F32),
        lback=per_sweep((n_region, piece, width), F32),
        yg=per_half((n_tile, half, width), BF16),
        eg=per_half((n_link, half, width), BF16),
        cout=per_half((n_link, half, width), F32),
        cin=per_half((n_link, half, width), F32),
        rout=per_half((5, 2, half, width), F32),
        rin=per_half((5, 2, half, width), F32),
        rnear=per_half((7, half, width), F32),
        rdir=per_half((6, half, width), F32),
    )

    def body(ins, out, moved_out, scr):
        kernel(n_region, n_tile, n_link, out, moved_out, types.SimpleNamespace(**ins, **scr))

    packed, moved = pl.pallas_call(
        body,
        out_shape=(results, moved),
        in_specs=({k: v[1] for k, v in inputs.items()},),
        out_specs=(vmem, vmem),
        scratch_shapes=(scratch,),
        compiler_params=pltpu.CompilerParams(
            collective_id=0, has_side_effects=True, vmem_limit_bytes=VMEM_LIMIT
        ),
        cost_estimate=pl.CostEstimate(flops=80_000_000, bytes_accessed=2_000_000, transcendentals=0),
        name="pdhg",
    )({k: v[0] for k, v in inputs.items()})

    def split(src, row, *rest):
        outs, moved_cut, sem = rest[:8], rest[8], rest[9]
        copies = [pltpu.make_async_copy(src.at[i], outs[i], sem.at[i]) for i in range(8)]
        for c in copies:
            c.start()
        moved_cut[...] = row[:, :scen]
        for c in copies:
            c.wait()

    one = jax.ShapeDtypeStruct((scen, width), F32)
    *outs, cut = pl.pallas_call(
        split,
        out_shape=[one] * 8 + [jax.ShapeDtypeStruct((1, scen), F32)],
        in_specs=[vmem, vmem],
        out_specs=[anywhere] * 8 + [vmem],
        scratch_shapes=[pltpu.SemaphoreType.DMA((8,))],
        name="split",
    )(packed, moved)
    return (*outs, cut.reshape(scen))


def solution(mesh):
    blocked = P(None, SPLIT)
    shared = P(None, LINK)
    tiled = P(REGION, TILE, LINK)
    slabs = P(REGION, TILE, LINK, None, None)
    states = (blocked, shared, blocked, shared)
    return jax.shard_map(
        on_device,
        mesh=mesh,
        in_specs=(
            slabs, tiled, tiled, tiled, slabs, tiled, P(SPLIT), P(LINK), blocked, P(LINK),
            *states, *states, P(), P(), P(), P(),
        ),
        out_specs=(*states, *states, P()),
        check_vma=False,
    )
```

```python
import types

import jax
import jax.numpy as jnp
from jax import lax
from jax.experimental import pallas as pl
from jax.experimental.pallas import tpu as pltpu
from jax.sharding import PartitionSpec as P

REGION, TILE, LINK = SPLIT = ("region", "tile", "link")
MESH = pl.DeviceIdType.MESH
F32 = jnp.float32
BF16 = jnp.bfloat16
HALVES = 2
SWEEPS = 2
NEAR = (1, -1, 2, -2)
FAR = 5
N_SEMS = 360
LANES = 128
TOP = 32766.0
I16 = jnp.int16
VMEM_LIMIT = 62 * 1024 * 1024
Z_PARTNERS = (FAR, -FAR, 3, -3, 2, -2, 1, -1)


def dot_nn(a, b):
    return lax.dot_general(a, b, (((1,), (0,)), ((), ())), preferred_element_type=F32)


def dot_nt(a, b):
    return lax.dot_general(a, b, (((1,), (1,)), ((), ())), preferred_element_type=F32)


def kernel(n_region, n_tile, n_link, out, moved_out, refs):
    r, t, l = lax.axis_index(REGION), lax.axis_index(TILE), lax.axis_index(LINK)
    tile_row, tile_col, tile_count, linkage_block = refs.rows, refs.cols, refs.count, refs.target
    scen, width = refs.y.shape[1:]
    slots = refs.tiles_v.shape[0]
    half = scen // HALVES
    piece = scen // n_region
    ssem, rsem = refs.ssem, refs.rsem
    used = [0]
    sent = []

    def z_dev(offset):
        return (r, lax.rem(t + (offset + n_tile), n_tile), l)

    def link_dev(offset):
        return (r, t, lax.rem(l + offset, n_link))

    def region_dev(offset):
        return (lax.rem(r + offset, n_region), t, l)

    def send(src, dst, dev):
        i = used[0]
        used[0] = i + 1
        assert i < N_SEMS
        c = pltpu.make_async_remote_copy(
            src_ref=src, dst_ref=dst, send_sem=ssem.at[i], recv_sem=rsem.at[i], device_id=dev, device_id_type=MESH
        )
        c.start()
        sent.append(c)
        return c

    barrier = pltpu.get_barrier_semaphore()
    for o in Z_PARTNERS:
        pl.semaphore_signal(barrier, inc=1, device_id=z_dev(o), device_id_type=MESH)
    for o in range(1, n_link):
        pl.semaphore_signal(barrier, inc=1, device_id=link_dev(o), device_id_type=MESH)
    for o in range(1, n_region):
        pl.semaphore_signal(barrier, inc=1, device_id=region_dev(o), device_id_type=MESH)

    def load(i, src, dst):
        c = pltpu.make_async_copy(src, dst, refs.lsem.at[i])
        c.start()
        return c

    duals_loads = [load(0, refs.duals_now, refs.duals_now_v), load(1, refs.duals_mean, refs.duals_mean_v)]
    linkage_loads = [load(2, refs.linkage_now, refs.linkage_now_v), load(3, refs.linkage_mean, refs.linkage_mean_v)]
    other_loads = [
        load(4, refs.tiles, refs.tiles_v),
        load(5, refs.ltile, refs.ltile_v),
        load(6, refs.demand, refs.demand_v),
        load(7, refs.primal_now, refs.primal_now_v),
        load(8, refs.primal_mean, refs.primal_mean_v),
        load(9, refs.capacity_now, refs.capacity_now_v),
        load(10, refs.capacity_mean, refs.capacity_mean_v),
    ]

    eye = lax.broadcasted_iota(jnp.int32, (scen, scen), 0) == lax.broadcasted_iota(jnp.int32, (scen, scen), 1)

    def column(row):
        return jnp.sum(jnp.where(eye, jnp.broadcast_to(row, (scen, scen)), 0.0), axis=1, keepdims=True)

    restart_row = refs.restart[...].astype(F32)
    restarted = jnp.broadcast_to(column(restart_row), (scen, width)) == 1.0
    weight = jnp.broadcast_to(column(refs.mean_count[...].astype(F32) * (1.0 - restart_row)), (scen, width))
    step_p = jnp.broadcast_to(column(refs.primal_step[...]), (scen, width))
    step_d = jnp.broadcast_to(column(refs.dual_step[...]), (scen, width))

    def part(value, h):
        return value[h * half : (h + 1) * half]

    def rows_of(h):
        return pl.ds(h * half, half)

    live = tile_count[0, 0, 0]
    row_at, col_at = [], []
    for k in range(slots):
        dead = jnp.where(k < live, 0, -64)
        row_at.append(lax.rem(tile_row[0, 0, k] - t + n_tile, n_tile) + dead)
        col_at.append(lax.rem(tile_col[0, 0, k] - l + n_link, n_link) + dead)
    row_slot = [lax.rem(tile_row[0, 0, k] - t + n_tile, n_tile) for k in range(slots)]
    col_slot = [lax.rem(tile_col[0, 0, k] - l + n_link, n_link) for k in range(slots)]
    target_at = lax.rem(linkage_block[0, 0, 0] - l + n_link, n_link)

    x, y, z, w = refs.x, refs.y, refs.z, refs.w
    for c in duals_loads:
        c.wait()
    y[0] = jnp.where(restarted, refs.duals_mean_v[...], refs.duals_now_v[...])
    for h in range(HALVES):
        refs.yg[0][h][0] = y[0, rows_of(h), :].astype(BF16)
    for c in linkage_loads:
        c.wait()
    w[0] = jnp.where(restarted, refs.linkage_mean_v[...], refs.linkage_now_v[...])
    refs.wg[0][0] = w[0].astype(BF16)

    pl.semaphore_wait(barrier, len(Z_PARTNERS) + n_link - 1 + n_region - 1)

    def duals_send(s, h):
        g = refs.yg[s][h]
        out = {}
        for d in (FAR, -FAR) + NEAR:
            slot = -d % n_tile
            out[slot] = send(g.at[0], g.at[slot], z_dev(d))
        return out

    def duals_forward(s, h, out):
        g = refs.yg[s][h]
        order = (-3, -2, -1, 1, 2) if h == 0 else (-2, -1, 1, 2)
        back = (3, 2, 1, -1, -2) if h == 1 else (2, 1, -1, -2)
        for slot, moves in ((FAR, order), (n_tile - FAR, back)):
            out.pop(slot).wait_recv()
            for d in moves:
                to = (slot - d) % n_tile
                out[to] = send(g.at[slot], g.at[to], z_dev(d))

    def link_gather(buf):
        out = []
        for d in range(1, n_link):
            out.append(send(buf.at[0], buf.at[-d % n_link], link_dev(d)))
        return out

    def finish(copies):
        for c in copies:
            c.wait_recv()

    def picked(at, terms, offset):
        total = None
        for k in range(slots):
            one = jnp.where(at[k] == offset, 1.0, 0.0) * terms[k]
            total = one if total is None else total + one
        return total

    def lane_top(value, top):
        value = jnp.abs(value)
        for i in range(0, width, LANES):
            top = jnp.maximum(top, jnp.max(value[:, i : i + LANES], axis=0, keepdims=True))
        return top

    def wide(row):
        return jnp.concatenate([row] * (width // LANES), axis=1)

    def fixed(value, inverse):
        return jnp.round(value * inverse).astype(jnp.int32).astype(I16)

    def loose(value, scale):
        return value.astype(jnp.int32).astype(F32) * wide(scale)

    least = jnp.full((1, LANES), 1e-30, F32)

    def columns_send(s, h):
        g = refs.yg[s][h]
        terms = [dot_nn(g[row_slot[k]], refs.tiles_v[k]) for k in range(slots)]
        parts, out, scale = refs.cpart[s][h], refs.cout[s][h], refs.cscale_out[s][h]
        top = least
        for o in range(n_link):
            parts[o] = picked(col_at, terms, o)
            top = lane_top(parts[o], top)
        scale[...] = top * (1.0 / TOP)
        inverse = wide(TOP / top)
        copies = []
        for o in range(1, n_link):
            copies.append(send(scale, refs.cscale[s][h].at[o], link_dev(o)))
            out[o] = fixed(parts[o], inverse)
            copies.append(send(out.at[o], refs.cin[s][h].at[o], link_dev(o)))
        return copies

    def primal_update(s, h):
        total = refs.cpart[s][h][0]
        for o in range(1, n_link):
            total = total + loose(refs.cin[s][h][o], refs.cscale[s][h][o])
        linked = refs.wg[s][target_at]
        gradient = total - dot_nn(part(linked, h), refs.ltile_v[...])
        old = x[s, rows_of(h), :]
        new = jnp.maximum(old - part(step_p, h) * (refs.column_cost[...] - gradient), 0.0)
        x[s + 1, rows_of(h), :] = new
        extrap = (2.0 * new - old).astype(BF16)
        refs.eg[s][h][0] = extrap

    def rows_send(s, h):
        g = refs.eg[s][h]
        terms = [dot_nt(g[col_slot[k]], refs.tiles_v[k]) for k in range(slots)]
        parts, out, near, scale = refs.rpart[s][h], refs.rout[s][h], refs.rnear[s][h], refs.rscale_out[s][h]
        top = least
        for o in range(n_tile):
            parts[o] = picked(row_at, terms, o)
            top = lane_top(parts[o], top)
        scale[...] = top * (1.0 / TOP)
        inverse = wide(TOP / top)
        third = 3 if h == 0 else -3
        copies = []
        for i, e in enumerate(NEAR):
            copies.append(send(scale, refs.rscale[s][h].at[i], z_dev(-e)))
            out[i, 0] = fixed(parts[(-e - FAR) % n_tile], inverse)
            out[i, 1] = fixed(parts[(-e + FAR) % n_tile], inverse)
            copies.append(send(out.at[i], refs.rin[s][h].at[i], z_dev(-e)))
            if i == 0:
                copies.append(send(scale, refs.rscale[s][h].at[4], z_dev(-third)))
                out[4, 0] = fixed(parts[n_tile // 2], inverse)
                copies.append(send(out.at[4, 0], refs.rin[s][h].at[4, 0], z_dev(-third)))
        for i, e in enumerate(NEAR):
            near[i] = fixed(parts[-e % n_tile], inverse)
        return copies

    def rows_direct(s, h):
        return [
            send(refs.rnear[s][h].at[i], refs.rdir[s][h].at[i], z_dev(-e)) for i, e in enumerate(NEAR)
        ]

    def rows_relay(s, h, copies):
        finish(copies)
        got, parts, scale = refs.rin[s][h], refs.rpart[s][h], refs.rscale[s][h]
        totals, top = [], least
        for j in range(2):
            total = parts[FAR if j else n_tile - FAR]
            for i in range(4):
                total = total + loose(got[i, j], scale[i])
            if j == h:
                total = total + loose(got[4, 0], scale[4])
            totals.append(total)
            top = lane_top(total, top)
        refs.fscale_out[s][h][...] = top * (1.0 / TOP)
        inverse = wide(TOP / top)
        result = []
        for j in range(2):
            to = z_dev(FAR if j else -FAR)
            result.append(send(refs.fscale_out[s][h], refs.fscale[s][h].at[j], to))
            refs.rfar[s][h][j] = fixed(totals[j], inverse)
            result.append(send(refs.rfar[s][h].at[j], refs.rfin[s][h].at[j], to))
        return result

    def duals_update(s, h, copies):
        finish(copies)
        total = refs.rpart[s][h][0]
        for i in range(4):
            total = total + loose(refs.rdir[s][h][i], refs.rscale[s][h][i])
        for j in range(2):
            total = total + loose(refs.rfin[s][h][j], refs.fscale[s][h][j])
        rows = rows_of(h)
        new = jnp.maximum(y[s, rows, :] + part(step_d, h) * (refs.demand_v[rows, :] - total), 0.0)
        y[s + 1, rows, :] = new
        if s + 1 < SWEEPS:
            refs.yg[s + 1][h][0] = new.astype(BF16)

    def linking_start(s):
        out = refs.lout[s]
        e = jnp.concatenate([refs.eg[s][h][0] for h in range(HALVES)], axis=0)
        term = dot_nt(e, refs.ltile_v[...])
        top = lane_top(term, least)
        refs.lscale_out[s][...] = top * (1.0 / TOP)
        scaled = term * wide(TOP / top)
        refs.lsum[s][...] = jnp.where(target_at == 0, 1.0, 0.0) * term
        copies = []
        for o in range(1, n_link):
            copies.append(send(refs.lscale_out[s], refs.lscale[s].at[o], link_dev(o)))
            out[o] = fixed(scaled, jnp.where(target_at == o, 1.0, 0.0))
            copies.append(send(out.at[o], refs.lin[s].at[o], link_dev(o)))
        return copies

    def linking_region(s, copies):
        finish(copies)
        total = refs.lsum[s][...]
        for o in range(1, n_link):
            total = total + loose(refs.lin[s][o], refs.lscale[s][o])
        own = refs.lsum[s]
        own[...] = total
        got = refs.lreg[s]
        result = []
        for o in range(1, n_region):
            to = lax.rem(r + o, n_region)
            rows = pl.ds(pl.multiple_of(to * piece, piece), piece)
            result.append(send(own.at[rows, :], got.at[r], region_dev(o)))
        got[r] = own[pl.ds(pl.multiple_of(r * piece, piece), piece), :]
        return result

    def summed(ref, n):
        total = ref[0]
        for i in range(1, n):
            total = total + ref[i]
        return total

    def spread(buf, at, value, devs):
        buf[at] = value
        return [send(buf.at[at], buf.at[at], d) for d in devs]

    region_devs = [region_dev(o) for o in range(1, n_region)]
    link_devs = [link_dev(o) for o in range(1, n_link)]

    def z_spread(buf, value):
        buf[t] = value
        return {d: send(buf.at[t], buf.at[t], z_dev(-d)) for d in (FAR, -FAR) + NEAR}

    def z_relay(buf, out):
        for d, moves in ((FAR, (-3, -2, -1, 1, 2)), (-FAR, (2, 1, -1, -2))):
            out.pop(d).wait_recv()
            at = lax.rem(t + (d + n_tile), n_tile)
            for m in moves:
                out[d, m] = send(buf.at[at], buf.at[at], z_dev(m))

    def linking_z(s, copies):
        finish(copies)
        return z_spread(refs.lz[s], summed(refs.lreg[s], n_region))

    def linking_back(s, copies):
        finish(copies.values())
        return spread(refs.lback[s], r, summed(refs.lz[s], n_tile), region_devs)

    def capacity_update(s):
        z[s + 1] = jnp.maximum(z[s] - step_p * (refs.capacity_cost[...] - w[s]), 0.0)

    def linking_update(s, copies):
        finish(copies)
        back = refs.lback[s]
        total = jnp.concatenate([back[i] for i in range(n_region)], axis=0)
        bar = 2.0 * z[s + 1] - z[s]
        w[s + 1] = jnp.maximum(w[s] + step_d * (refs.linkage_bound[...] - (bar - total)), 0.0)

    def average(mean, state, i):
        out[i] = (weight * mean + state[1] + state[2]) / (weight + 2.0)

    ready = [duals_send(0, h) for h in range(HALVES)]
    w_copies = link_gather(refs.wg[0])
    for c in other_loads:
        c.wait()
    x[0] = jnp.where(restarted, refs.primal_mean_v[...], refs.primal_now_v[...])
    z[0] = jnp.where(restarted, refs.capacity_mean_v[...], refs.capacity_now_v[...])

    link_copies = None
    for s in range(SWEEPS):
        last = s + 1 == SWEEPS
        for h in range(HALVES):
            duals_forward(s, h, ready[h])
        if s:
            link_copies = linking_back(s - 1, link_copies)
        columns = []
        for h in range(HALVES):
            finish(ready[h].values())
            columns.append(columns_send(s, h))
        if s:
            linking_update(s - 1, link_copies)
            refs.wg[s][0] = w[s].astype(BF16)
            w_copies = link_gather(refs.wg[s])
        capacity_update(s)
        finish(w_copies)
        gathers = []
        for h in range(HALVES):
            finish(columns[h])
            primal_update(s, h)
            gathers.append(link_gather(refs.eg[s][h]))
        link_copies = linking_start(s)
        relays, directs = [], []
        for h in range(HALVES):
            finish(gathers[h])
            relays.append(rows_send(s, h))
        for h in range(HALVES):
            directs.append(rows_direct(s, h))
        link_copies = linking_region(s, link_copies)
        for h in range(HALVES):
            directs[h] += rows_relay(s, h, relays[h])
        link_copies = linking_z(s, link_copies)
        if last:
            out[0] = x[2]
            out[1] = z[2]
            average(refs.primal_mean_v[...], x, 4)
            average(refs.capacity_mean_v[...], z, 5)
        for h in range(HALVES):
            duals_update(s, h, directs[h])
            if not last:
                ready[h] = duals_send(s + 1, h)
        if not last:
            z_relay(refs.lz[s], link_copies)

    def squares(state):
        return jnp.sum((state[2] - state[0]) ** 2, axis=1, keepdims=True)

    def as_row(col):
        lanes = refs.mz.shape[-1]
        on = lax.broadcasted_iota(jnp.int32, (scen, lanes), 0) == lax.broadcasted_iota(jnp.int32, (scen, lanes), 1)
        return jnp.sum(jnp.where(on, jnp.broadcast_to(col, (scen, lanes)), 0.0), axis=0, keepdims=True)

    copies = z_spread(refs.mz, as_row(squares(x) + squares(y)))
    out[2] = y[2]
    average(refs.duals_mean_v[...], y, 6)
    z_relay(refs.lz[SWEEPS - 1], link_copies)
    z_relay(refs.mz, copies)
    link_copies = linking_back(SWEEPS - 1, link_copies)
    finish(copies.values())
    copies = spread(refs.mreg, r, summed(refs.mz, n_tile), region_devs)
    linking_update(SWEEPS - 1, link_copies)
    moved = as_row(squares(z) + squares(w))
    out[3] = w[2]
    average(refs.linkage_mean_v[...], w, 7)
    finish(copies)
    copies = spread(refs.mlink, l, summed(refs.mreg, n_region) + moved, link_devs)
    finish(copies)
    moved_out[...] = summed(refs.mlink, n_link)
    for c in sent:
        c.wait_send()


def on_device(
    tiles, tile_row, tile_col, tile_count, linkage_tiles, linkage_block, column_cost, capacity_cost, demand,
    linkage_bound, primal_now, capacity_now, duals_now, linkage_now, primal_mean, capacity_mean, duals_mean,
    linkage_mean, restart, mean_count, primal_step, dual_step,
):
    n_region, n_tile, n_link = (lax.axis_size(a) for a in SPLIT)
    scen, width = primal_now.shape
    slots = tile_row.shape[2]
    half = scen // HALVES
    piece = scen // n_region
    smem = pl.BlockSpec(memory_space=pltpu.SMEM)
    vmem = pl.BlockSpec(memory_space=pltpu.VMEM)
    hbm = pl.BlockSpec(memory_space=pltpu.HBM)
    anywhere = pl.BlockSpec(memory_space=pl.ANY)
    inputs = dict(
        rows=(tile_row, smem),
        cols=(tile_col, smem),
        count=(tile_count, smem),
        target=(linkage_block, smem),
        restart=(restart.reshape(1, scen), vmem),
        mean_count=(mean_count.reshape(1, scen), vmem),
        primal_step=(primal_step.reshape(1, scen), vmem),
        dual_step=(dual_step.reshape(1, scen), vmem),
        column_cost=(column_cost.reshape(1, width), vmem),
        capacity_cost=(capacity_cost.reshape(1, width), vmem),
        linkage_bound=(linkage_bound.reshape(1, width), vmem),
        tiles=(tiles.reshape(slots, width, width), hbm),
        ltile=(linkage_tiles.reshape(width, width), hbm),
        demand=(demand, hbm),
        primal_now=(primal_now, hbm),
        capacity_now=(capacity_now, hbm),
        duals_now=(duals_now, hbm),
        linkage_now=(linkage_now, hbm),
        primal_mean=(primal_mean, hbm),
        capacity_mean=(capacity_mean, hbm),
        duals_mean=(duals_mean, hbm),
        linkage_mean=(linkage_mean, hbm),
    )
    results = jax.ShapeDtypeStruct((8, scen, width), F32)
    moved = jax.ShapeDtypeStruct((1, 128), F32)
    block = pltpu.VMEM((scen, width), F32)

    def per_sweep(shape, dtype):
        return [pltpu.VMEM(shape, dtype)] * SWEEPS

    def per_half(shape, dtype):
        return [[pltpu.VMEM(shape, dtype)] * HALVES] * SWEEPS

    scratch = dict(
        ssem=pltpu.SemaphoreType.DMA((N_SEMS,)),
        rsem=pltpu.SemaphoreType.DMA((N_SEMS,)),
        lsem=pltpu.SemaphoreType.DMA((11,)),
        tiles_v=pltpu.VMEM((slots, width, width), BF16),
        ltile_v=pltpu.VMEM((width, width), BF16),
        mz=pltpu.VMEM((n_tile, 1, 128), F32),
        mreg=pltpu.VMEM((n_region, 1, 128), F32),
        mlink=pltpu.VMEM((n_link, 1, 128), F32),
        duals_now_v=block,
        duals_mean_v=block,
        linkage_now_v=block,
        linkage_mean_v=block,
        primal_now_v=block,
        primal_mean_v=block,
        capacity_now_v=block,
        capacity_mean_v=block,
        demand_v=block,
        x=pltpu.VMEM((SWEEPS + 1, scen, width), F32),
        y=pltpu.VMEM((SWEEPS + 1, scen, width), F32),
        z=pltpu.VMEM((SWEEPS + 1, scen, width), F32),
        w=pltpu.VMEM((SWEEPS + 1, scen, width), F32),
        wg=per_sweep((n_link, scen, width), BF16),
        lout=per_sweep((n_link, scen, width), I16),
        lin=per_sweep((n_link, scen, width), I16),
        lscale=per_sweep((n_link, 1, LANES), F32),
        lscale_out=per_sweep((1, LANES), F32),
        lsum=per_sweep((scen, width), F32),
        lreg=per_sweep((n_region, piece, width), F32),
        lz=per_sweep((n_tile, piece, width), F32),
        lback=per_sweep((n_region, piece, width), F32),
        yg=per_half((n_tile, half, width), BF16),
        eg=per_half((n_link, half, width), BF16),
        cpart=per_half((n_link, half, width), F32),
        cout=per_half((n_link, half, width), I16),
        cin=per_half((n_link, half, width), I16),
        cscale=per_half((n_link, 1, LANES), F32),
        cscale_out=per_half((1, LANES), F32),
        rpart=per_half((n_tile, half, width), F32),
        rout=per_half((5, 2, half, width), I16),
        rin=per_half((5, 2, half, width), I16),
        rscale=per_half((5, 1, LANES), F32),
        rscale_out=per_half((1, LANES), F32),
        rnear=per_half((4, half, width), I16),
        rdir=per_half((4, half, width), I16),
        rfar=per_half((2, half, width), I16),
        rfin=per_half((2, half, width), I16),
        fscale=per_half((2, 1, LANES), F32),
        fscale_out=per_half((1, LANES), F32),
    )

    def body(ins, out, moved_out, scr):
        kernel(n_region, n_tile, n_link, out, moved_out, types.SimpleNamespace(**ins, **scr))

    packed, moved = pl.pallas_call(
        body,
        out_shape=(results, moved),
        in_specs=({k: v[1] for k, v in inputs.items()},),
        out_specs=(vmem, vmem),
        scratch_shapes=(scratch,),
        compiler_params=pltpu.CompilerParams(
            collective_id=0, has_side_effects=True, vmem_limit_bytes=VMEM_LIMIT
        ),
        cost_estimate=pl.CostEstimate(flops=80_000_000, bytes_accessed=2_000_000, transcendentals=0),
        name="pdhg",
    )({k: v[0] for k, v in inputs.items()})

    def split(src, row, *rest):
        outs, moved_cut, sem = rest[:8], rest[8], rest[9]
        copies = [pltpu.make_async_copy(src.at[i], outs[i], sem.at[i]) for i in range(8)]
        for c in copies:
            c.start()
        moved_cut[...] = row[:, :scen]
        for c in copies:
            c.wait()

    one = jax.ShapeDtypeStruct((scen, width), F32)
    *outs, cut = pl.pallas_call(
        split,
        out_shape=[one] * 8 + [jax.ShapeDtypeStruct((1, scen), F32)],
        in_specs=[vmem, vmem],
        out_specs=[anywhere] * 8 + [vmem],
        scratch_shapes=[pltpu.SemaphoreType.DMA((8,))],
        name="split",
    )(packed, moved)
    return (*outs, cut.reshape(scen))


def solution(mesh):
    blocked = P(None, SPLIT)
    shared = P(None, LINK)
    tiled = P(REGION, TILE, LINK)
    slabs = P(REGION, TILE, LINK, None, None)
    states = (blocked, shared, blocked, shared)
    return jax.shard_map(
        on_device,
        mesh=mesh,
        in_specs=(
            slabs, tiled, tiled, tiled, slabs, tiled, P(SPLIT), P(LINK), blocked, P(LINK),
            *states, *states, P(), P(), P(), P(),
        ),
        out_specs=(*states, *states, P()),
        check_vma=False,
    )
```

```python
import types

import jax
import jax.numpy as jnp
from jax import lax
from jax.experimental import pallas as pl
from jax.experimental.pallas import tpu as pltpu
from jax.sharding import PartitionSpec as P

REGION, TILE, LINK = SPLIT = ("region", "tile", "link")
MESH = pl.DeviceIdType.MESH
F32 = jnp.float32
BF16 = jnp.bfloat16
HALVES = 2
SWEEPS = 2
NEAR = (1, -1, 2, -2)
FAR = 5
LINK_ORDER = (4, 3, 5, 2, 6, 1, 7)
N_SEMS = 360
LANES = 128
TOP = 32766.0
I16 = jnp.int16
VMEM_LIMIT = 62 * 1024 * 1024
Z_PARTNERS = (FAR, -FAR, 3, -3, 2, -2, 1, -1)


def dot_nn(a, b):
    return lax.dot_general(a, b, (((1,), (0,)), ((), ())), preferred_element_type=F32)


def dot_nt(a, b):
    return lax.dot_general(a, b, (((1,), (1,)), ((), ())), preferred_element_type=F32)


def kernel(n_region, n_tile, n_link, out, moved_out, refs):
    r, t, l = lax.axis_index(REGION), lax.axis_index(TILE), lax.axis_index(LINK)
    tile_row, tile_col, tile_count, linkage_block = refs.rows, refs.cols, refs.count, refs.target
    scen, width = refs.y.shape[1:]
    slots = refs.tiles_v.shape[0]
    half = scen // HALVES
    piece = scen // n_region
    ssem, rsem = refs.ssem, refs.rsem
    used = [0]
    sent = []

    def z_dev(offset):
        return (r, lax.rem(t + (offset + n_tile), n_tile), l)

    def link_dev(offset):
        return (r, t, lax.rem(l + offset, n_link))

    def region_dev(offset):
        return (lax.rem(r + offset, n_region), t, l)

    def send(src, dst, dev):
        i = used[0]
        used[0] = i + 1
        assert i < N_SEMS
        c = pltpu.make_async_remote_copy(
            src_ref=src, dst_ref=dst, send_sem=ssem.at[i], recv_sem=rsem.at[i], device_id=dev, device_id_type=MESH
        )
        c.start()
        sent.append(c)
        return c

    barrier = pltpu.get_barrier_semaphore()
    for o in Z_PARTNERS:
        pl.semaphore_signal(barrier, inc=1, device_id=z_dev(o), device_id_type=MESH)
    for o in range(1, n_link):
        pl.semaphore_signal(barrier, inc=1, device_id=link_dev(o), device_id_type=MESH)
    for o in range(1, n_region):
        pl.semaphore_signal(barrier, inc=1, device_id=region_dev(o), device_id_type=MESH)

    def load(i, src, dst):
        c = pltpu.make_async_copy(src, dst, refs.lsem.at[i])
        c.start()
        return c

    duals_loads = [load(0, refs.duals_now, refs.duals_now_v), load(1, refs.duals_mean, refs.duals_mean_v)]
    linkage_loads = [load(2, refs.linkage_now, refs.linkage_now_v), load(3, refs.linkage_mean, refs.linkage_mean_v)]
    other_loads = [
        load(4, refs.tiles, refs.tiles_v),
        load(5, refs.ltile, refs.ltile_v),
        load(6, refs.demand, refs.demand_v),
        load(7, refs.primal_now, refs.primal_now_v),
        load(8, refs.primal_mean, refs.primal_mean_v),
        load(9, refs.capacity_now, refs.capacity_now_v),
        load(10, refs.capacity_mean, refs.capacity_mean_v),
    ]

    eye = lax.broadcasted_iota(jnp.int32, (scen, scen), 0) == lax.broadcasted_iota(jnp.int32, (scen, scen), 1)

    def column(row):
        return jnp.sum(jnp.where(eye, jnp.broadcast_to(row, (scen, scen)), 0.0), axis=1, keepdims=True)

    restart_row = refs.restart[...].astype(F32)
    restarted = jnp.broadcast_to(column(restart_row), (scen, width)) == 1.0
    weight = jnp.broadcast_to(column(refs.mean_count[...].astype(F32) * (1.0 - restart_row)), (scen, width))
    step_p = jnp.broadcast_to(column(refs.primal_step[...]), (scen, width))
    step_d = jnp.broadcast_to(column(refs.dual_step[...]), (scen, width))

    def part(value, h):
        return value[h * half : (h + 1) * half]

    def rows_of(h):
        return pl.ds(h * half, half)

    live = tile_count[0, 0, 0]
    row_at, col_at = [], []
    for k in range(slots):
        dead = jnp.where(k < live, 0, -64)
        row_at.append(lax.rem(tile_row[0, 0, k] - t + n_tile, n_tile) + dead)
        col_at.append(lax.rem(tile_col[0, 0, k] - l + n_link, n_link) + dead)
    row_slot = [lax.rem(tile_row[0, 0, k] - t + n_tile, n_tile) for k in range(slots)]
    col_slot = [lax.rem(tile_col[0, 0, k] - l + n_link, n_link) for k in range(slots)]
    target_at = lax.rem(linkage_block[0, 0, 0] - l + n_link, n_link)

    x, y, z, w = refs.x, refs.y, refs.z, refs.w
    for c in duals_loads:
        c.wait()
    y[0] = jnp.where(restarted, refs.duals_mean_v[...], refs.duals_now_v[...])
    for h in range(HALVES):
        refs.yg[0][h][0] = y[0, rows_of(h), :].astype(BF16)
    for c in linkage_loads:
        c.wait()
    w[0] = jnp.where(restarted, refs.linkage_mean_v[...], refs.linkage_now_v[...])
    refs.wg[0][0] = w[0].astype(BF16)

    pl.semaphore_wait(barrier, len(Z_PARTNERS) + n_link - 1 + n_region - 1)

    def duals_send(s, h):
        g = refs.yg[s][h]
        out = {}
        for d in (FAR, -FAR) + NEAR:
            slot = -d % n_tile
            out[slot] = send(g.at[0], g.at[slot], z_dev(d))
        return out

    def duals_forward(s, h, out):
        g = refs.yg[s][h]
        order = (-3, -2, -1, 1, 2) if h == 0 else (-2, -1, 1, 2)
        back = (3, 2, 1, -1, -2) if h == 1 else (2, 1, -1, -2)
        for slot, moves in ((FAR, order), (n_tile - FAR, back)):
            out.pop(slot).wait_recv()
            for d in moves:
                to = (slot - d) % n_tile
                out[to] = send(g.at[slot], g.at[to], z_dev(d))

    def link_gather(buf):
        out = []
        for d in LINK_ORDER:
            out.append(send(buf.at[0], buf.at[-d % n_link], link_dev(d)))
        return out

    def finish(copies):
        for c in copies:
            c.wait_recv()

    def picked(at, terms, offset):
        total = None
        for k in range(slots):
            one = jnp.where(at[k] == offset, 1.0, 0.0) * terms[k]
            total = one if total is None else total + one
        return total

    def lane_top(value, top):
        value = jnp.abs(value)
        for i in range(0, width, LANES):
            top = jnp.maximum(top, jnp.max(value[:, i : i + LANES], axis=0, keepdims=True))
        return top

    def wide(row):
        return jnp.concatenate([row] * (width // LANES), axis=1)

    def fixed(value, inverse):
        return jnp.round(value * inverse).astype(jnp.int32).astype(I16)

    def loose(value, scale):
        return value.astype(jnp.int32).astype(F32) * wide(scale)

    least = jnp.full((1, LANES), 1e-30, F32)

    def columns_send(s, h):
        g = refs.yg[s][h]
        terms = [dot_nn(g[row_slot[k]], refs.tiles_v[k]) for k in range(slots)]
        out = refs.cout[s][h]
        copies = []
        for o in LINK_ORDER + (0,):
            out[o] = picked(col_at, terms, o)
            if o:
                copies.append(send(out.at[o], refs.cin[s][h].at[o], link_dev(o)))
        return copies

    def primal_update(s, h):
        total = refs.cout[s][h][0]
        for o in range(1, n_link):
            total = total + refs.cin[s][h][o]
        linked = refs.wg[s][target_at]
        gradient = total - dot_nn(part(linked, h), refs.ltile_v[...])
        old = x[s, rows_of(h), :]
        new = jnp.maximum(old - part(step_p, h) * (refs.column_cost[...] - gradient), 0.0)
        x[s + 1, rows_of(h), :] = new
        extrap = (2.0 * new - old).astype(BF16)
        refs.eg[s][h][0] = extrap

    def rows_send(s, h):
        g = refs.eg[s][h]
        terms = [dot_nt(g[col_slot[k]], refs.tiles_v[k]) for k in range(slots)]
        parts, out, near, scale = refs.rpart[s][h], refs.rout[s][h], refs.rnear[s][h], refs.rscale_out[s][h]
        top = least
        for o in range(n_tile):
            parts[o] = picked(row_at, terms, o)
            top = lane_top(parts[o], top)
        scale[...] = top * (1.0 / TOP)
        inverse = wide(TOP / top)
        third = 3 if h == 0 else -3
        copies = []
        for i, e in enumerate(NEAR):
            copies.append(send(scale, refs.rscale[s][h].at[i], z_dev(-e)))
            out[i, 0] = fixed(parts[(-e - FAR) % n_tile], inverse)
            out[i, 1] = fixed(parts[(-e + FAR) % n_tile], inverse)
            copies.append(send(out.at[i], refs.rin[s][h].at[i], z_dev(-e)))
            if i == 0:
                copies.append(send(scale, refs.rscale[s][h].at[4], z_dev(-third)))
                out[4, 0] = fixed(parts[n_tile // 2], inverse)
                copies.append(send(out.at[4, 0], refs.rin[s][h].at[4, 0], z_dev(-third)))
        for i, e in enumerate(NEAR):
            near[i] = fixed(parts[-e % n_tile], inverse)
        return copies

    def rows_direct(s, h):
        return [
            send(refs.rnear[s][h].at[i], refs.rdir[s][h].at[i], z_dev(-e)) for i, e in enumerate(NEAR)
        ]

    def rows_relay(s, h, copies):
        finish(copies)
        got, parts, scale = refs.rin[s][h], refs.rpart[s][h], refs.rscale[s][h]
        totals, top = [], least
        for j in range(2):
            total = parts[FAR if j else n_tile - FAR]
            for i in range(4):
                total = total + loose(got[i, j], scale[i])
            if j == h:
                total = total + loose(got[4, 0], scale[4])
            totals.append(total)
            top = lane_top(total, top)
        refs.fscale_out[s][h][...] = top * (1.0 / TOP)
        inverse = wide(TOP / top)
        result = []
        for j in range(2):
            to = z_dev(FAR if j else -FAR)
            result.append(send(refs.fscale_out[s][h], refs.fscale[s][h].at[j], to))
            refs.rfar[s][h][j] = fixed(totals[j], inverse)
            result.append(send(refs.rfar[s][h].at[j], refs.rfin[s][h].at[j], to))
        return result

    def duals_update(s, h, copies):
        finish(copies)
        total = refs.rpart[s][h][0]
        for i in range(4):
            total = total + loose(refs.rdir[s][h][i], refs.rscale[s][h][i])
        for j in range(2):
            total = total + loose(refs.rfin[s][h][j], refs.fscale[s][h][j])
        rows = rows_of(h)
        new = jnp.maximum(y[s, rows, :] + part(step_d, h) * (refs.demand_v[rows, :] - total), 0.0)
        y[s + 1, rows, :] = new
        if s + 1 < SWEEPS:
            refs.yg[s + 1][h][0] = new.astype(BF16)

    def linking_start(s):
        out = refs.lout[s]
        e = jnp.concatenate([refs.eg[s][h][0] for h in range(HALVES)], axis=0)
        term = dot_nt(e, refs.ltile_v[...])
        top = lane_top(term, least)
        refs.lscale_out[s][...] = top * (1.0 / TOP)
        scaled = term * wide(TOP / top)
        refs.lsum[s][...] = jnp.where(target_at == 0, 1.0, 0.0) * term
        copies = []
        for o in LINK_ORDER:
            copies.append(send(refs.lscale_out[s], refs.lscale[s].at[o], link_dev(o)))
            out[o] = fixed(scaled, jnp.where(target_at == o, 1.0, 0.0))
            copies.append(send(out.at[o], refs.lin[s].at[o], link_dev(o)))
        return copies

    def linking_region(s, copies):
        finish(copies)
        total = refs.lsum[s][...]
        for o in range(1, n_link):
            total = total + loose(refs.lin[s][o], refs.lscale[s][o])
        own = refs.lsum[s]
        own[...] = total
        got = refs.lreg[s]
        result = []
        for o in range(1, n_region):
            to = lax.rem(r + o, n_region)
            rows = pl.ds(pl.multiple_of(to * piece, piece), piece)
            result.append(send(own.at[rows, :], got.at[r], region_dev(o)))
        got[r] = own[pl.ds(pl.multiple_of(r * piece, piece), piece), :]
        return result

    def summed(ref, n):
        total = ref[0]
        for i in range(1, n):
            total = total + ref[i]
        return total

    def spread(buf, at, value, devs):
        buf[at] = value
        return [send(buf.at[at], buf.at[at], d) for d in devs]

    region_devs = [region_dev(o) for o in range(1, n_region)]
    link_devs = [link_dev(o) for o in LINK_ORDER]

    def z_spread(buf, value):
        buf[t] = value
        return {d: send(buf.at[t], buf.at[t], z_dev(-d)) for d in (FAR, -FAR) + NEAR}

    def z_relay(buf, out):
        for d, moves in ((FAR, (-3, -2, -1, 1, 2)), (-FAR, (2, 1, -1, -2))):
            out.pop(d).wait_recv()
            at = lax.rem(t + (d + n_tile), n_tile)
            for m in moves:
                out[d, m] = send(buf.at[at], buf.at[at], z_dev(m))

    def linking_z(s, copies):
        finish(copies)
        return z_spread(refs.lz[s], summed(refs.lreg[s], n_region))

    def linking_back(s, copies):
        finish(copies.values())
        return spread(refs.lback[s], r, summed(refs.lz[s], n_tile), region_devs)

    def capacity_update(s):
        z[s + 1] = jnp.maximum(z[s] - step_p * (refs.capacity_cost[...] - w[s]), 0.0)

    def linking_update(s, copies):
        finish(copies)
        back = refs.lback[s]
        total = jnp.concatenate([back[i] for i in range(n_region)], axis=0)
        bar = 2.0 * z[s + 1] - z[s]
        w[s + 1] = jnp.maximum(w[s] + step_d * (refs.linkage_bound[...] - (bar - total)), 0.0)

    stores = []

    def store(i, value):
        refs.result[i] = value
        c = pltpu.make_async_copy(refs.result.at[i], out.at[i], refs.osem.at[i])
        c.start()
        stores.append(c)

    def average(mean, state, i):
        store(i, (weight * mean + state[1] + state[2]) / (weight + 2.0))

    ready = [duals_send(0, h) for h in range(HALVES)]
    w_copies = link_gather(refs.wg[0])
    for c in other_loads:
        c.wait()
    x[0] = jnp.where(restarted, refs.primal_mean_v[...], refs.primal_now_v[...])
    z[0] = jnp.where(restarted, refs.capacity_mean_v[...], refs.capacity_now_v[...])

    link_copies = None
    for s in range(SWEEPS):
        last = s + 1 == SWEEPS
        for h in range(HALVES):
            duals_forward(s, h, ready[h])
        if s:
            link_copies = linking_back(s - 1, link_copies)
        columns = []
        for h in range(HALVES):
            finish(ready[h].values())
            columns.append(columns_send(s, h))
        if s:
            linking_update(s - 1, link_copies)
            refs.wg[s][0] = w[s].astype(BF16)
            w_copies = link_gather(refs.wg[s])
        capacity_update(s)
        finish(w_copies)
        gathers = []
        for h in range(HALVES):
            finish(columns[h])
            primal_update(s, h)
            gathers.append(link_gather(refs.eg[s][h]))
        link_copies = linking_start(s)
        relays, directs = [], []
        for h in range(HALVES):
            finish(gathers[h])
            relays.append(rows_send(s, h))
        for h in range(HALVES):
            directs.append(rows_direct(s, h))
        link_copies = linking_region(s, link_copies)
        for h in range(HALVES):
            directs[h] += rows_relay(s, h, relays[h])
        link_copies = linking_z(s, link_copies)
        if last:
            store(0, x[2])
            store(1, z[2])
            average(refs.primal_mean_v[...], x, 4)
            average(refs.capacity_mean_v[...], z, 5)
        for h in range(HALVES):
            duals_update(s, h, directs[h])
            if not last:
                ready[h] = duals_send(s + 1, h)
        if not last:
            z_relay(refs.lz[s], link_copies)

    def squares(state):
        return jnp.sum((state[2] - state[0]) ** 2, axis=1, keepdims=True)

    def as_row(col):
        lanes = refs.mz.shape[-1]
        on = lax.broadcasted_iota(jnp.int32, (scen, lanes), 0) == lax.broadcasted_iota(jnp.int32, (scen, lanes), 1)
        return jnp.sum(jnp.where(on, jnp.broadcast_to(col, (scen, lanes)), 0.0), axis=0, keepdims=True)

    copies = z_spread(refs.mz, as_row(squares(x) + squares(y)))
    store(2, y[2])
    average(refs.duals_mean_v[...], y, 6)
    z_relay(refs.lz[SWEEPS - 1], link_copies)
    z_relay(refs.mz, copies)
    link_copies = linking_back(SWEEPS - 1, link_copies)
    finish(copies.values())
    copies = spread(refs.mreg, r, summed(refs.mz, n_tile), region_devs)
    linking_update(SWEEPS - 1, link_copies)
    moved = as_row(squares(z) + squares(w))
    store(3, w[2])
    average(refs.linkage_mean_v[...], w, 7)
    finish(copies)
    copies = spread(refs.mlink, l, summed(refs.mreg, n_region) + moved, link_devs)
    finish(copies)
    moved_out[...] = summed(refs.mlink, n_link)
    for c in sent:
        c.wait_send()
    for c in stores:
        c.wait()


def on_device(
    tiles, tile_row, tile_col, tile_count, linkage_tiles, linkage_block, column_cost, capacity_cost, demand,
    linkage_bound, primal_now, capacity_now, duals_now, linkage_now, primal_mean, capacity_mean, duals_mean,
    linkage_mean, restart, mean_count, primal_step, dual_step,
):
    n_region, n_tile, n_link = (lax.axis_size(a) for a in SPLIT)
    scen, width = primal_now.shape
    slots = tile_row.shape[2]
    half = scen // HALVES
    piece = scen // n_region
    smem = pl.BlockSpec(memory_space=pltpu.SMEM)
    vmem = pl.BlockSpec(memory_space=pltpu.VMEM)
    hbm = pl.BlockSpec(memory_space=pltpu.HBM)
    anywhere = pl.BlockSpec(memory_space=pl.ANY)
    inputs = dict(
        rows=(tile_row, smem),
        cols=(tile_col, smem),
        count=(tile_count, smem),
        target=(linkage_block, smem),
        restart=(restart.reshape(1, scen), vmem),
        mean_count=(mean_count.reshape(1, scen), vmem),
        primal_step=(primal_step.reshape(1, scen), vmem),
        dual_step=(dual_step.reshape(1, scen), vmem),
        column_cost=(column_cost.reshape(1, width), vmem),
        capacity_cost=(capacity_cost.reshape(1, width), vmem),
        linkage_bound=(linkage_bound.reshape(1, width), vmem),
        tiles=(tiles.reshape(slots, width, width), hbm),
        ltile=(linkage_tiles.reshape(width, width), hbm),
        demand=(demand, hbm),
        primal_now=(primal_now, hbm),
        capacity_now=(capacity_now, hbm),
        duals_now=(duals_now, hbm),
        linkage_now=(linkage_now, hbm),
        primal_mean=(primal_mean, hbm),
        capacity_mean=(capacity_mean, hbm),
        duals_mean=(duals_mean, hbm),
        linkage_mean=(linkage_mean, hbm),
    )
    results = jax.ShapeDtypeStruct((8, scen, width), F32)
    moved = jax.ShapeDtypeStruct((1, 128), F32)
    block = pltpu.VMEM((scen, width), F32)

    def per_sweep(shape, dtype):
        return [pltpu.VMEM(shape, dtype)] * SWEEPS

    def per_half(shape, dtype):
        return [[pltpu.VMEM(shape, dtype)] * HALVES] * SWEEPS

    scratch = dict(
        ssem=pltpu.SemaphoreType.DMA((N_SEMS,)),
        rsem=pltpu.SemaphoreType.DMA((N_SEMS,)),
        lsem=pltpu.SemaphoreType.DMA((11,)),
        osem=pltpu.SemaphoreType.DMA((8,)),
        result=pltpu.VMEM((8, scen, width), F32),
        tiles_v=pltpu.VMEM((slots, width, width), BF16),
        ltile_v=pltpu.VMEM((width, width), BF16),
        mz=pltpu.VMEM((n_tile, 1, 128), F32),
        mreg=pltpu.VMEM((n_region, 1, 128), F32),
        mlink=pltpu.VMEM((n_link, 1, 128), F32),
        duals_now_v=block,
        duals_mean_v=block,
        linkage_now_v=block,
        linkage_mean_v=block,
        primal_now_v=block,
        primal_mean_v=block,
        capacity_now_v=block,
        capacity_mean_v=block,
        demand_v=block,
        x=pltpu.VMEM((SWEEPS + 1, scen, width), F32),
        y=pltpu.VMEM((SWEEPS + 1, scen, width), F32),
        z=pltpu.VMEM((SWEEPS + 1, scen, width), F32),
        w=pltpu.VMEM((SWEEPS + 1, scen, width), F32),
        wg=per_sweep((n_link, scen, width), BF16),
        lout=per_sweep((n_link, scen, width), I16),
        lin=per_sweep((n_link, scen, width), I16),
        lscale=per_sweep((n_link, 1, LANES), F32),
        lscale_out=per_sweep((1, LANES), F32),
        lsum=per_sweep((scen, width), F32),
        lreg=per_sweep((n_region, piece, width), F32),
        lz=per_sweep((n_tile, piece, width), F32),
        lback=per_sweep((n_region, piece, width), F32),
        yg=per_half((n_tile, half, width), BF16),
        eg=per_half((n_link, half, width), BF16),
        cout=per_half((n_link, half, width), F32),
        cin=per_half((n_link, half, width), F32),
        rpart=per_half((n_tile, half, width), F32),
        rout=per_half((5, 2, half, width), I16),
        rin=per_half((5, 2, half, width), I16),
        rscale=per_half((5, 1, LANES), F32),
        rscale_out=per_half((1, LANES), F32),
        rnear=per_half((4, half, width), I16),
        rdir=per_half((4, half, width), I16),
        rfar=per_half((2, half, width), I16),
        rfin=per_half((2, half, width), I16),
        fscale=per_half((2, 1, LANES), F32),
        fscale_out=per_half((1, LANES), F32),
    )

    def body(ins, out, moved_out, scr):
        kernel(n_region, n_tile, n_link, out, moved_out, types.SimpleNamespace(**ins, **scr))

    packed, moved = pl.pallas_call(
        body,
        out_shape=(results, moved),
        in_specs=({k: v[1] for k, v in inputs.items()},),
        out_specs=(hbm, vmem),
        scratch_shapes=(scratch,),
        compiler_params=pltpu.CompilerParams(
            collective_id=0, has_side_effects=True, vmem_limit_bytes=VMEM_LIMIT
        ),
        cost_estimate=pl.CostEstimate(flops=80_000_000, bytes_accessed=2_000_000, transcendentals=0),
        name="pdhg",
    )({k: v[0] for k, v in inputs.items()})

    def split(src, row, *rest):
        outs, moved_cut, sem = rest[:8], rest[8], rest[9]
        copies = [pltpu.make_async_copy(src.at[i], outs[i], sem.at[i]) for i in range(8)]
        for c in copies:
            c.start()
        moved_cut[...] = row[:, :scen]
        for c in copies:
            c.wait()

    one = jax.ShapeDtypeStruct((scen, width), F32)
    *outs, cut = pl.pallas_call(
        split,
        out_shape=[one] * 8 + [jax.ShapeDtypeStruct((1, scen), F32)],
        in_specs=[vmem, vmem],
        out_specs=[anywhere] * 8 + [vmem],
        scratch_shapes=[pltpu.SemaphoreType.DMA((8,))],
        name="split",
    )(packed, moved)
    return (*outs, cut.reshape(scen))


def solution(mesh):
    blocked = P(None, SPLIT)
    shared = P(None, LINK)
    tiled = P(REGION, TILE, LINK)
    slabs = P(REGION, TILE, LINK, None, None)
    states = (blocked, shared, blocked, shared)
    return jax.shard_map(
        on_device,
        mesh=mesh,
        in_specs=(
            slabs, tiled, tiled, tiled, slabs, tiled, P(SPLIT), P(LINK), blocked, P(LINK),
            *states, *states, P(), P(), P(), P(),
        ),
        out_specs=(*states, *states, P()),
        check_vma=False,
    )
```

```python
import types

import jax
import jax.numpy as jnp
from jax import lax
from jax.experimental import pallas as pl
from jax.experimental.pallas import tpu as pltpu
from jax.sharding import PartitionSpec as P

REGION, TILE, LINK = SPLIT = ("region", "tile", "link")
MESH = pl.DeviceIdType.MESH
F32 = jnp.float32
BF16 = jnp.bfloat16
HALVES = 2
SWEEPS = 2
NEAR = (2, -2, 1, -1)
FAR = 5
LINK_ORDER = (4, 3, 5, 2, 6, 1, 7)
N_SEMS = 360
LANES = 128
TOP = 32766.0
I16 = jnp.int16
VMEM_LIMIT = 62 * 1024 * 1024
Z_PARTNERS = (FAR, -FAR, 3, -3, 2, -2, 1, -1)


def dot_nn(a, b):
    return lax.dot_general(a, b, (((1,), (0,)), ((), ())), preferred_element_type=F32)


def dot_nt(a, b):
    return lax.dot_general(a, b, (((1,), (1,)), ((), ())), preferred_element_type=F32)


def kernel(n_region, n_tile, n_link, out, moved_out, refs):
    r, t, l = lax.axis_index(REGION), lax.axis_index(TILE), lax.axis_index(LINK)
    tile_row, tile_col, tile_count, linkage_block = refs.rows, refs.cols, refs.count, refs.target
    scen, width = refs.y.shape[1:]
    slots = refs.tiles_v.shape[0]
    half = scen // HALVES
    piece = scen // n_region
    ssem, rsem = refs.ssem, refs.rsem
    used = [0]
    sent = []

    def z_dev(offset):
        return (r, lax.rem(t + (offset + n_tile), n_tile), l)

    def link_dev(offset):
        return (r, t, lax.rem(l + offset, n_link))

    def region_dev(offset):
        return (lax.rem(r + offset, n_region), t, l)

    def send(src, dst, dev):
        i = used[0]
        used[0] = i + 1
        assert i < N_SEMS
        c = pltpu.make_async_remote_copy(
            src_ref=src, dst_ref=dst, send_sem=ssem.at[i], recv_sem=rsem.at[i], device_id=dev, device_id_type=MESH
        )
        c.start()
        sent.append(c)
        return c

    barrier = pltpu.get_barrier_semaphore()
    for o in Z_PARTNERS:
        pl.semaphore_signal(barrier, inc=1, device_id=z_dev(o), device_id_type=MESH)
    plane_devs = [
        (lax.rem(r + i, n_region), t, lax.rem(l + j, n_link))
        for i in range(n_region)
        for j in LINK_ORDER + (0,)
        if i or j
    ]
    for d in plane_devs:
        pl.semaphore_signal(barrier, inc=1, device_id=d, device_id_type=MESH)

    def load(i, src, dst):
        c = pltpu.make_async_copy(src, dst, refs.lsem.at[i])
        c.start()
        return c

    duals_loads = [load(0, refs.duals_now, refs.duals_now_v), load(1, refs.duals_mean, refs.duals_mean_v)]
    small_loads = [
        load(11, refs.restart, refs.restart_v),
        load(12, refs.mean_count, refs.mean_count_v),
        load(13, refs.primal_step, refs.primal_step_v),
        load(14, refs.dual_step, refs.dual_step_v),
    ]
    linkage_loads = [load(2, refs.linkage_now, refs.linkage_now_v), load(3, refs.linkage_mean, refs.linkage_mean_v)]
    other_loads = [
        load(4, refs.tiles, refs.tiles_v),
        load(5, refs.ltile, refs.ltile_v),
        load(6, refs.demand, refs.demand_v),
        load(7, refs.primal_now, refs.primal_now_v),
        load(8, refs.primal_mean, refs.primal_mean_v),
        load(9, refs.capacity_now, refs.capacity_now_v),
        load(10, refs.capacity_mean, refs.capacity_mean_v),
        load(15, refs.column_cost, refs.column_cost_v),
        load(16, refs.capacity_cost, refs.capacity_cost_v),
        load(17, refs.linkage_bound, refs.linkage_bound_v),
    ]

    eye = lax.broadcasted_iota(jnp.int32, (scen, scen), 0) == lax.broadcasted_iota(jnp.int32, (scen, scen), 1)

    def column(row):
        return jnp.sum(jnp.where(eye, jnp.broadcast_to(row, (scen, scen)), 0.0), axis=1, keepdims=True)

    for c in small_loads:
        c.wait()
    restart_row = refs.restart_v[...].astype(F32)
    restarted = jnp.broadcast_to(column(restart_row), (scen, width)) == 1.0
    weight = jnp.broadcast_to(column(refs.mean_count_v[...].astype(F32) * (1.0 - restart_row)), (scen, width))
    step_p = jnp.broadcast_to(column(refs.primal_step_v[...]), (scen, width))
    step_d = jnp.broadcast_to(column(refs.dual_step_v[...]), (scen, width))

    def part(value, h):
        return value[h * half : (h + 1) * half]

    def rows_of(h):
        return pl.ds(h * half, half)

    live = tile_count[0, 0, 0]
    row_at, col_at = [], []
    for k in range(slots):
        dead = jnp.where(k < live, 0, -64)
        row_at.append(lax.rem(tile_row[0, 0, k] - t + n_tile, n_tile) + dead)
        col_at.append(lax.rem(tile_col[0, 0, k] - l + n_link, n_link) + dead)
    row_slot = [lax.rem(tile_row[0, 0, k] - t + n_tile, n_tile) for k in range(slots)]
    col_slot = [lax.rem(tile_col[0, 0, k] - l + n_link, n_link) for k in range(slots)]
    target_at = lax.rem(linkage_block[0, 0, 0] - l + n_link, n_link)

    x, y, z, w = refs.x, refs.y, refs.z, refs.w
    for c in duals_loads:
        c.wait()
    y[0] = jnp.where(restarted, refs.duals_mean_v[...], refs.duals_now_v[...])
    for h in range(HALVES):
        refs.yg[0][h][0] = y[0, rows_of(h), :].astype(BF16)
    for c in linkage_loads:
        c.wait()
    w[0] = jnp.where(restarted, refs.linkage_mean_v[...], refs.linkage_now_v[...])
    refs.wg[0][0] = w[0].astype(BF16)

    pl.semaphore_wait(barrier, len(Z_PARTNERS) + len(plane_devs))

    def duals_send(s, h):
        g = refs.yg[s][h]
        out = {}
        for d in (FAR, -FAR) + NEAR:
            slot = -d % n_tile
            out[slot] = send(g.at[0], g.at[slot], z_dev(d))
        return out

    def duals_forward(s, h, out):
        g = refs.yg[s][h]
        order = (-3, -2, 2, -1, 1) if h == 0 else (-2, 2, -1, 1)
        back = (3, 2, -2, 1, -1) if h == 1 else (2, -2, 1, -1)
        for slot, moves in ((FAR, order), (n_tile - FAR, back)):
            out.pop(slot).wait_recv()
            for d in moves:
                to = (slot - d) % n_tile
                out[to] = send(g.at[slot], g.at[to], z_dev(d))

    def link_gather(buf):
        out = []
        for d in LINK_ORDER:
            out.append(send(buf.at[0], buf.at[-d % n_link], link_dev(d)))
        return out

    def finish(copies):
        for c in copies:
            c.wait_recv()

    def picked(at, terms, offset):
        total = None
        for k in range(slots):
            one = jnp.where(at[k] == offset, 1.0, 0.0) * terms[k]
            total = one if total is None else total + one
        return total

    def folded(value, top):
        value = jnp.abs(value)
        for i in range(0, width, LANES):
            lanes = value[:, i : i + LANES]
            top = lanes if top is None else jnp.maximum(top, lanes)
        return top

    def lane_top(values):
        top = None
        for value in values:
            top = folded(value, top)
        return jnp.maximum(jnp.max(top, axis=0, keepdims=True), 1e-30)

    def wide(row):
        return jnp.concatenate([row] * (width // LANES), axis=1)

    def fixed(value, inverse):
        return jnp.round(value * inverse).astype(jnp.int32).astype(I16)

    def loose(value, scale):
        return value.astype(jnp.int32).astype(F32) * wide(scale)

    def columns_send(s, h):
        g = refs.yg[s][h]
        terms = [dot_nn(g[row_slot[k]], refs.tiles_v[k]) for k in range(slots)]
        out = refs.cout[s][h]
        copies = []
        for o in LINK_ORDER + (0,):
            out[o] = picked(col_at, terms, o)
            if o:
                copies.append(send(out.at[o], refs.cin[s][h].at[o], link_dev(o)))
        return copies

    def primal_update(s, h):
        total = refs.cout[s][h][0]
        for o in range(1, n_link):
            total = total + refs.cin[s][h][o]
        linked = refs.wg[s][target_at]
        gradient = total - dot_nn(part(linked, h), refs.ltile_v[...])
        old = x[s, rows_of(h), :]
        new = jnp.maximum(old - part(step_p, h) * (refs.column_cost_v[...] - gradient), 0.0)
        x[s + 1, rows_of(h), :] = new
        extrap = (2.0 * new - old).astype(BF16)
        refs.eg[s][h][0] = extrap

    def rows_send(s, h):
        g = refs.eg[s][h]
        terms = [dot_nt(g[col_slot[k]], refs.tiles_v[k]) for k in range(slots)]
        parts, out, near, scale = refs.rpart[s][h], refs.rout[s][h], refs.rnear[s][h], refs.rscale_out[s][h]
        top = None
        for o in range(n_tile):
            one = picked(row_at, terms, o)
            parts[o] = one
            top = folded(one, top)
        top = jnp.maximum(jnp.max(top, axis=0, keepdims=True), 1e-30)
        scale[...] = top * (1.0 / TOP)
        inverse = wide(TOP / top)
        third = 3 if h == 0 else -3
        copies = [send(scale, refs.rscale[s][h].at[4], z_dev(-third))]
        out[4, 0] = fixed(parts[n_tile // 2], inverse)
        copies.append(send(out.at[4, 0], refs.rin[s][h].at[4, 0], z_dev(-third)))
        for i, e in enumerate(NEAR):
            copies.append(send(scale, refs.rscale[s][h].at[i], z_dev(-e)))
            out[i, 0] = fixed(parts[(-e - FAR) % n_tile], inverse)
            out[i, 1] = fixed(parts[(-e + FAR) % n_tile], inverse)
            copies.append(send(out.at[i], refs.rin[s][h].at[i], z_dev(-e)))
        for i, e in enumerate(NEAR):
            near[i] = fixed(parts[-e % n_tile], inverse)
        return copies

    def rows_direct(s, h):
        return [
            send(refs.rnear[s][h].at[i], refs.rdir[s][h].at[i], z_dev(-e)) for i, e in enumerate(NEAR)
        ]

    def rows_relay(s, h, copies):
        finish(copies)
        got, parts, scale = refs.rin[s][h], refs.rpart[s][h], refs.rscale[s][h]
        totals = []
        for j in range(2):
            total = parts[FAR if j else n_tile - FAR]
            for i in range(4):
                total = total + loose(got[i, j], scale[i])
            if j == h:
                total = total + loose(got[4, 0], scale[4])
            totals.append(total)
        top = lane_top(totals)
        refs.fscale_out[s][h][...] = top * (1.0 / TOP)
        inverse = wide(TOP / top)
        result = []
        for j in range(2):
            to = z_dev(FAR if j else -FAR)
            result.append(send(refs.fscale_out[s][h], refs.fscale[s][h].at[j], to))
            refs.rfar[s][h][j] = fixed(totals[j], inverse)
            result.append(send(refs.rfar[s][h].at[j], refs.rfin[s][h].at[j], to))
        return result

    def duals_update(s, h, copies):
        finish(copies)
        total = refs.rpart[s][h][0]
        for i in range(4):
            total = total + loose(refs.rdir[s][h][i], refs.rscale[s][h][i])
        for j in range(2):
            total = total + loose(refs.rfin[s][h][j], refs.fscale[s][h][j])
        rows = rows_of(h)
        new = jnp.maximum(y[s, rows, :] + part(step_d, h) * (refs.demand_v[rows, :] - total), 0.0)
        y[s + 1, rows, :] = new
        if s + 1 < SWEEPS:
            refs.yg[s + 1][h][0] = new.astype(BF16)

    def linking_start(s):
        out = refs.lout[s]
        e = jnp.concatenate([refs.eg[s][h][0] for h in range(HALVES)], axis=0)
        term = dot_nt(e, refs.ltile_v[...])
        top = lane_top([term])
        refs.lscale_out[s][...] = top * (1.0 / TOP)
        scaled = term * wide(TOP / top)
        refs.lsum[s][...] = jnp.where(target_at == 0, 1.0, 0.0) * term
        copies = []
        for o in LINK_ORDER:
            copies.append(send(refs.lscale_out[s], refs.lscale[s].at[o], link_dev(o)))
            out[o] = fixed(scaled, jnp.where(target_at == o, 1.0, 0.0))
            copies.append(send(out.at[o], refs.lin[s].at[o], link_dev(o)))
        return copies

    def linking_region(s, copies):
        finish(copies)
        total = refs.lsum[s][...]
        for o in range(1, n_link):
            total = total + loose(refs.lin[s][o], refs.lscale[s][o])
        own = refs.lsum[s]
        own[...] = total
        got = refs.lreg[s]
        result = []
        for o in range(1, n_region):
            to = lax.rem(r + o, n_region)
            rows = pl.ds(pl.multiple_of(to * piece, piece), piece)
            result.append(send(own.at[rows, :], got.at[r], region_dev(o)))
        got[r] = own[pl.ds(pl.multiple_of(r * piece, piece), piece), :]
        return result

    def summed(ref, n):
        total = ref[0]
        for i in range(1, n):
            total = total + ref[i]
        return total

    def spread(buf, at, value, devs):
        buf[at] = value
        return [send(buf.at[at], buf.at[at], d) for d in devs]

    region_devs = [region_dev(o) for o in range(1, n_region)]
    link_devs = [link_dev(o) for o in LINK_ORDER]

    def z_spread(buf, value):
        buf[t] = value
        return {d: send(buf.at[t], buf.at[t], z_dev(-d)) for d in (FAR, -FAR) + NEAR}

    def z_relay(buf, out):
        for d, moves in ((FAR, (-3, -2, 2, -1, 1)), (-FAR, (2, -2, 1, -1))):
            out.pop(d).wait_recv()
            at = lax.rem(t + (d + n_tile), n_tile)
            for m in moves:
                out[d, m] = send(buf.at[at], buf.at[at], z_dev(m))

    def linking_z(s, copies):
        finish(copies)
        return z_spread(refs.lz[s], summed(refs.lreg[s], n_region))

    def linking_back(s, copies):
        finish(copies.values())
        return spread(refs.lback[s], r, summed(refs.lz[s], n_tile), region_devs)

    def capacity_update(s):
        z[s + 1] = jnp.maximum(z[s] - step_p * (refs.capacity_cost_v[...] - w[s]), 0.0)

    def linking_update(s, copies):
        finish(copies)
        back = refs.lback[s]
        total = jnp.concatenate([back[i] for i in range(n_region)], axis=0)
        bar = 2.0 * z[s + 1] - z[s]
        w[s + 1] = jnp.maximum(w[s] + step_d * (refs.linkage_bound_v[...] - (bar - total)), 0.0)

    stores = []

    def store(i, value):
        refs.result[i] = value
        c = pltpu.make_async_copy(refs.result.at[i], out.at[i], refs.osem.at[i])
        c.start()
        stores.append(c)

    def average(mean, state, i):
        store(i, (weight * mean + state[1] + state[2]) / (weight + 2.0))

    ready = [duals_send(0, h) for h in range(HALVES)]
    w_copies = link_gather(refs.wg[0])
    for c in other_loads:
        c.wait()
    x[0] = jnp.where(restarted, refs.primal_mean_v[...], refs.primal_now_v[...])
    z[0] = jnp.where(restarted, refs.capacity_mean_v[...], refs.capacity_now_v[...])

    link_copies = None
    for s in range(SWEEPS):
        last = s + 1 == SWEEPS
        for h in range(HALVES):
            duals_forward(s, h, ready[h])
        if s:
            link_copies = linking_back(s - 1, link_copies)
        if s:
            linking_update(s - 1, link_copies)
            refs.wg[s][0] = w[s].astype(BF16)
            w_copies = link_gather(refs.wg[s])
        columns = []
        for h in range(HALVES):
            finish(ready[h].values())
            columns.append(columns_send(s, h))
        capacity_update(s)
        finish(w_copies)
        gathers = []
        for h in range(HALVES):
            finish(columns[h])
            primal_update(s, h)
            gathers.append(link_gather(refs.eg[s][h]))
        link_copies = linking_start(s)
        relays, directs = [], []
        for h in range(HALVES):
            finish(gathers[h])
            relays.append(rows_send(s, h))
        for h in range(HALVES):
            directs.append(rows_direct(s, h))
        link_copies = linking_region(s, link_copies)
        for h in range(HALVES):
            directs[h] += rows_relay(s, h, relays[h])
            if h == 0:
                link_copies = linking_z(s, link_copies)
        if last:
            store(0, x[2])
            store(1, z[2])
            average(refs.primal_mean_v[...], x, 4)
            average(refs.capacity_mean_v[...], z, 5)
        for h in range(HALVES):
            duals_update(s, h, directs[h])
            if not last:
                ready[h] = duals_send(s + 1, h)
        if not last:
            z_relay(refs.lz[s], link_copies)

    def squares(state):
        return jnp.sum((state[2] - state[0]) ** 2, axis=1, keepdims=True)

    def as_row(col):
        lanes = refs.mz.shape[-1]
        on = lax.broadcasted_iota(jnp.int32, (scen, lanes), 0) == lax.broadcasted_iota(jnp.int32, (scen, lanes), 1)
        return jnp.sum(jnp.where(on, jnp.broadcast_to(col, (scen, lanes)), 0.0), axis=0, keepdims=True)

    copies = z_spread(refs.mz, as_row(squares(x) + squares(y)))
    store(2, y[2])
    average(refs.duals_mean_v[...], y, 6)
    z_relay(refs.lz[SWEEPS - 1], link_copies)
    z_relay(refs.mz, copies)
    link_copies = linking_back(SWEEPS - 1, link_copies)
    linking_update(SWEEPS - 1, link_copies)
    moved = jnp.where(r == 0, 1.0, 0.0) * as_row(squares(z) + squares(w))
    finish(copies.values())
    copies = spread(refs.mplane, r * n_link + l, summed(refs.mz, n_tile) + moved, plane_devs)
    store(3, w[2])
    average(refs.linkage_mean_v[...], w, 7)
    finish(copies)
    moved_out[...] = summed(refs.mplane, n_region * n_link)
    for c in sent:
        c.wait_send()
    for c in stores:
        c.wait()


def on_device(
    tiles, tile_row, tile_col, tile_count, linkage_tiles, linkage_block, column_cost, capacity_cost, demand,
    linkage_bound, primal_now, capacity_now, duals_now, linkage_now, primal_mean, capacity_mean, duals_mean,
    linkage_mean, restart, mean_count, primal_step, dual_step,
):
    n_region, n_tile, n_link = (lax.axis_size(a) for a in SPLIT)
    scen, width = primal_now.shape
    slots = tile_row.shape[2]
    half = scen // HALVES
    piece = scen // n_region
    smem = pl.BlockSpec(memory_space=pltpu.SMEM)
    vmem = pl.BlockSpec(memory_space=pltpu.VMEM)
    hbm = pl.BlockSpec(memory_space=pltpu.HBM)
    anywhere = pl.BlockSpec(memory_space=pl.ANY)
    inputs = dict(
        rows=(tile_row, smem),
        cols=(tile_col, smem),
        count=(tile_count, smem),
        target=(linkage_block, smem),
        restart=(restart.reshape(1, scen), hbm),
        mean_count=(mean_count.reshape(1, scen), hbm),
        primal_step=(primal_step.reshape(1, scen), hbm),
        dual_step=(dual_step.reshape(1, scen), hbm),
        column_cost=(column_cost.reshape(1, width), hbm),
        capacity_cost=(capacity_cost.reshape(1, width), hbm),
        linkage_bound=(linkage_bound.reshape(1, width), hbm),
        tiles=(tiles.reshape(slots, width, width), hbm),
        ltile=(linkage_tiles.reshape(width, width), hbm),
        demand=(demand, hbm),
        primal_now=(primal_now, hbm),
        capacity_now=(capacity_now, hbm),
        duals_now=(duals_now, hbm),
        linkage_now=(linkage_now, hbm),
        primal_mean=(primal_mean, hbm),
        capacity_mean=(capacity_mean, hbm),
        duals_mean=(duals_mean, hbm),
        linkage_mean=(linkage_mean, hbm),
    )
    results = jax.ShapeDtypeStruct((8, scen, width), F32)
    moved = jax.ShapeDtypeStruct((1, 128), F32)
    block = pltpu.VMEM((scen, width), F32)

    def per_sweep(shape, dtype):
        return [pltpu.VMEM(shape, dtype)] * SWEEPS

    def per_half(shape, dtype):
        return [[pltpu.VMEM(shape, dtype)] * HALVES] * SWEEPS

    scratch = dict(
        ssem=pltpu.SemaphoreType.DMA((N_SEMS,)),
        rsem=pltpu.SemaphoreType.DMA((N_SEMS,)),
        lsem=pltpu.SemaphoreType.DMA((18,)),
        osem=pltpu.SemaphoreType.DMA((8,)),
        result=pltpu.VMEM((8, scen, width), F32),
        tiles_v=pltpu.VMEM((slots, width, width), BF16),
        ltile_v=pltpu.VMEM((width, width), BF16),
        mz=pltpu.VMEM((n_tile, 1, 128), F32),
        mplane=pltpu.VMEM((n_region * n_link, 1, 128), F32),
        restart_v=pltpu.VMEM((1, scen), jnp.int32),
        mean_count_v=pltpu.VMEM((1, scen), jnp.int32),
        primal_step_v=pltpu.VMEM((1, scen), F32),
        dual_step_v=pltpu.VMEM((1, scen), F32),
        column_cost_v=pltpu.VMEM((1, width), F32),
        capacity_cost_v=pltpu.VMEM((1, width), F32),
        linkage_bound_v=pltpu.VMEM((1, width), F32),
        duals_now_v=block,
        duals_mean_v=block,
        linkage_now_v=block,
        linkage_mean_v=block,
        primal_now_v=block,
        primal_mean_v=block,
        capacity_now_v=block,
        capacity_mean_v=block,
        demand_v=block,
        x=pltpu.VMEM((SWEEPS + 1, scen, width), F32),
        y=pltpu.VMEM((SWEEPS + 1, scen, width), F32),
        z=pltpu.VMEM((SWEEPS + 1, scen, width), F32),
        w=pltpu.VMEM((SWEEPS + 1, scen, width), F32),
        wg=per_sweep((n_link, scen, width), BF16),
        lout=per_sweep((n_link, scen, width), I16),
        lin=per_sweep((n_link, scen, width), I16),
        lscale=per_sweep((n_link, 1, LANES), F32),
        lscale_out=per_sweep((1, LANES), F32),
        lsum=per_sweep((scen, width), F32),
        lreg=per_sweep((n_region, piece, width), F32),
        lz=per_sweep((n_tile, piece, width), F32),
        lback=per_sweep((n_region, piece, width), F32),
        yg=per_half((n_tile, half, width), BF16),
        eg=per_half((n_link, half, width), BF16),
        cout=per_half((n_link, half, width), F32),
        cin=per_half((n_link, half, width), F32),
        rpart=per_half((n_tile, half, width), F32),
        rout=per_half((5, 2, half, width), I16),
        rin=per_half((5, 2, half, width), I16),
        rscale=per_half((5, 1, LANES), F32),
        rscale_out=per_half((1, LANES), F32),
        rnear=per_half((4, half, width), I16),
        rdir=per_half((4, half, width), I16),
        rfar=per_half((2, half, width), I16),
        rfin=per_half((2, half, width), I16),
        fscale=per_half((2, 1, LANES), F32),
        fscale_out=per_half((1, LANES), F32),
    )

    def body(ins, out, moved_out, scr):
        kernel(n_region, n_tile, n_link, out, moved_out, types.SimpleNamespace(**ins, **scr))

    packed, moved = pl.pallas_call(
        body,
        out_shape=(results, moved),
        in_specs=({k: v[1] for k, v in inputs.items()},),
        out_specs=(hbm, vmem),
        scratch_shapes=(scratch,),
        compiler_params=pltpu.CompilerParams(
            collective_id=0, has_side_effects=True, vmem_limit_bytes=VMEM_LIMIT
        ),
        cost_estimate=pl.CostEstimate(flops=80_000_000, bytes_accessed=2_000_000, transcendentals=0),
        name="pdhg",
    )({k: v[0] for k, v in inputs.items()})

    def split(src, row, *rest):
        outs, moved_cut, sem = rest[:8], rest[8], rest[9]
        copies = [pltpu.make_async_copy(src.at[i], outs[i], sem.at[i]) for i in range(8)]
        for c in copies:
            c.start()
        moved_cut[...] = row[:, :scen]
        for c in copies:
            c.wait()

    one = jax.ShapeDtypeStruct((scen, width), F32)
    *outs, cut = pl.pallas_call(
        split,
        out_shape=[one] * 8 + [jax.ShapeDtypeStruct((1, scen), F32)],
        in_specs=[vmem, vmem],
        out_specs=[anywhere] * 8 + [vmem],
        scratch_shapes=[pltpu.SemaphoreType.DMA((8,))],
        name="split",
    )(packed, moved)
    return (*outs, cut.reshape(scen))


def solution(mesh):
    blocked = P(None, SPLIT)
    shared = P(None, LINK)
    tiled = P(REGION, TILE, LINK)
    slabs = P(REGION, TILE, LINK, None, None)
    states = (blocked, shared, blocked, shared)
    return jax.shard_map(
        on_device,
        mesh=mesh,
        in_specs=(
            slabs, tiled, tiled, tiled, slabs, tiled, P(SPLIT), P(LINK), blocked, P(LINK),
            *states, *states, P(), P(), P(), P(),
        ),
        out_specs=(*states, *states, P()),
        check_vma=False,
    )
```
